256 devices in a mesh: row: 8 (over y, z_lo), col: 32 (over x, z_hi, core).
Axes of the slice: x: 4, y: 4, z: 8 (z_hi: 4, z_lo: 2; z = z_hi * 2 + z_lo), core: 2. Of those that a mesh axis runs over, the one named last changes fastest.
Arguments:
- object_field: float32 [2, 2048, 8192], P(None, 'row', 'col'), may hold values from -5 to 5
- probe: float32 [2, 2, 256, 256], replicated, may hold values from -5 to 5
- amplitudes: float32 [8, 32, 1, 256, 256], P('row', 'col'), may hold values from 0.5 to 3
- offsets: int32 [8, 32, 1, 2], P('row', 'col'), may hold values from 0 to 128
Outputs:
- new_object: float32 [2, 2048, 8192], P(None, 'row', 'col')
- new_probe: float32 [2, 2, 256, 256], replicated
The draws below stay inside these ranges and needn't reach their ends.
All inputs are finite; a program needn't handle non-finite values.
Results may differ from the reference program's by a relative error of at most 0.0003.
Values sent between devices are 32-bit elements; how exact they have to be, the bound alone decides.
No kernel may reach another device: no remote copies, remote signals or barrier semaphores. Data moves between devices by JAX's collectives and lax.ppermute only.
A program may use at most 64 MiB of HBM per device.

```python
import jax
import jax.numpy as jnp
from jax import lax

TILE = 256
H = 64
F = 256
M = 2
POS = 1
ITERS = 2
NR = 2048
NC = 8192
N_ROW = 8
N_COL = 32


def plant(values, own_key, low, high):
    index_at = [jax.random.randint(jax.random.fold_in(own_key, axis), (), 0, length) for axis, length in enumerate(values.shape)]
    main_axis = values.shape.index(max(values.shape))
    neighbour = index_at[:main_axis] + [(index_at[main_axis] + 1) % values.shape[main_axis]] + index_at[main_axis + 1:]
    return values.at[tuple(index_at)].set(low).at[tuple(neighbour)].set(high)


def levels(own_key, extent, cuts, smallest, largest):
    loudness = 1.0
    for position, shards_of in cuts:
        steps = jax.random.uniform(jax.random.fold_in(jax.random.fold_in(own_key, 6), position), (shards_of,), jnp.float32, smallest / len(cuts), largest / len(cuts))
        loudness = loudness * jnp.repeat(jnp.exp(steps), extent[position] // shards_of).reshape((-1,) + (1,) * (len(extent) - 1 - position))
    return loudness


def bell_draw(own_key, shape, deviation, reach, cuts=(), kind=jnp.bfloat16):
    values = deviation * jax.random.normal(own_key, shape, jnp.float32)
    if cuts:
        values = values * levels(own_key, shape, cuts, -0.22, 0.18)
    return jnp.clip(values, -reach, reach).astype(kind)


def setup_inputs(seed: int = 0) -> dict:
    splits = jax.random.split(jax.random.key(seed), 5)
    object_field = bell_draw(splits[0], (2, NR, NC), 0.7, 5.0, ((1, 8), (2, 32)), jnp.float32)
    probe = bell_draw(splits[1], (2, M, F, F), 0.7, 5.0, (), jnp.float32)
    amplitudes = jnp.clip(0.5 + 2.5 * jax.random.uniform(splits[2], (N_ROW, N_COL, POS, F, F), jnp.float32) ** levels(splits[2], (N_ROW, N_COL, POS, F, F), ((0, 8), (1, 32)), -0.2, 0.2), 0.5, 3.0)
    offsets = plant(jax.random.randint(splits[3], (N_ROW, N_COL, POS, 2), 0, TILE + 2 * H - F + 1), jax.random.fold_in(splits[3], 1), 0, TILE + 2 * H - F).astype(jnp.int32)
    return dict(object_field=object_field, probe=probe, amplitudes=amplitudes, offsets=offsets)


object_step = 0.25
probe_step = 4.0

def transform(real_part, imag_part, inverse):
    field = lax.complex(real_part, imag_part)
    if inverse:
        result = jnp.fft.ifft2(field, norm='ortho')
    else:
        result = jnp.fft.fft2(field, norm='ortho')
    return (jnp.real(result), jnp.imag(result))

def frame_terms(patch, probe, measured):
    probe_re, probe_im = (probe[0], probe[1])
    wave_re = probe_re * patch[0] - probe_im * patch[1]
    wave_im = probe_re * patch[1] + probe_im * patch[0]
    far_re, far_im = transform(wave_re, wave_im, False)
    intensity = lax.optimization_barrier(jnp.sum(far_re * far_re + far_im * far_im, axis=0))
    factor = 1.0 - measured / jnp.sqrt(intensity + 1.0)
    back_re, back_im = transform(far_re * factor, far_im * factor, True)
    object_re = lax.optimization_barrier(jnp.sum(probe_re * back_re + probe_im * back_im, axis=0))
    object_im = lax.optimization_barrier(jnp.sum(probe_re * back_im - probe_im * back_re, axis=0))
    probe_term_re = patch[0] * back_re + patch[1] * back_im
    probe_term_im = patch[0] * back_im - patch[1] * back_re
    return (jnp.stack([object_re, object_im]), jnp.stack([probe_term_re, probe_term_im]))

def reference(object_field, probe, amplitudes, offsets):
    frames = POS * N_ROW * N_COL
    row_base = (jnp.arange(N_ROW, dtype=jnp.int32) * TILE)[:, None, None]
    col_base = (jnp.arange(N_COL, dtype=jnp.int32) * TILE)[None, :, None]
    rows_at = (row_base + offsets[:, :, :, 0]).reshape(-1).astype(jnp.int32)
    cols_at = (col_base + offsets[:, :, :, 1]).reshape(-1).astype(jnp.int32)
    measured_all = amplitudes.reshape(-1, F, F)
    zero = jnp.zeros((), jnp.int32)

    def one_iteration(current, probes):
        padded = jnp.pad(current, ((0, 0), (H, H), (H, H)))

        def visit(carry, item):
            grad_pad, probe_grad = carry
            row_at, col_at, measured = item
            start = (zero, row_at.astype(jnp.int32), col_at.astype(jnp.int32))
            patch = lax.dynamic_slice(padded, start, (2, F, F))
            term_object, term_probe = frame_terms(patch, probes, measured)
            window = lax.dynamic_slice(grad_pad, start, (2, F, F))
            grad_pad = lax.dynamic_update_slice(grad_pad, window + term_object, start)
            return ((grad_pad, probe_grad + term_probe), None)
        (grad_pad, probe_grad), _ = lax.scan(visit, (jnp.zeros_like(padded), jnp.zeros_like(probes)), (rows_at, cols_at, measured_all))
        object_grad = grad_pad[:, H:H + NR, H:H + NC]
        return (current - object_step * object_grad, probes - probe_step / frames * probe_grad)
    current, probes = (object_field, probe)
    for iteration in range(ITERS):
        current, probes = one_iteration(current, probes)
    return (current, probes)
```

```python
import functools
import math

import jax
import jax.numpy as jnp
import ml_dtypes
import numpy as np
from jax import lax
from jax.experimental import pallas as pl
from jax.experimental.pallas import tpu as pltpu
from jax.sharding import PartitionSpec as P

H = 64
F = 256
M = 2
TILE = 256
SPAN = TILE + 2 * H
B = 2 * H
object_step = 0.25
probe_step = 4.0
RC = ("row", "col")
BIT_Y, BIT_ZLO, BIT_X, BIT_ZHI, BIT_CORE = 192, 32, 24, 6, 1

f32 = jnp.float32
bf16 = jnp.bfloat16
VMEM_LIMIT = 56 * 1024 * 1024
SMALL_LIMIT = 24 * 1024 * 1024


def tables():
    counter = np.arange(F)
    angle = -2.0 * math.pi / F * (counter[:, None] * counter[None, :] % F)
    out = []
    for table in (np.cos(angle) / math.sqrt(F), np.sin(angle) / math.sqrt(F)):
        high = table.astype(np.float32).astype(ml_dtypes.bfloat16)
        low = (table - high.astype(np.float64)).astype(np.float32).astype(ml_dtypes.bfloat16)
        out += [high, low]
    return np.concatenate(out, axis=0)


def blocks(table):
    rh, rl, ih, il = (table[k * F:(k + 1) * F, :] for k in range(4))

    def block(re, im, under):
        return jnp.concatenate(
            [jnp.concatenate([re, im], axis=1), jnp.concatenate([under, re], axis=1)], axis=0)

    return (block(rh, ih, -ih), block(rl, il, -il)), (block(rh, -ih, ih), block(rl, -il, il))


def split(x):
    high = x.astype(bf16)
    return high, (x - high.astype(f32)).astype(bf16)


def dot(a, b):
    return jnp.dot(a, b, preferred_element_type=f32)


def product(left, right):
    return dot(left[0], right[0]) + (dot(left[0], right[1]) + dot(left[1], right[0]))


LANE = 128


def lanes():
    return lax.broadcasted_iota(jnp.int32, (TILE, LANE), 1) < H


def half_turn(x):
    return pltpu.roll(x, H, 1)


def sides_kernel(obj, left, right):
    low = lanes()
    left[...] = jnp.where(low, obj[0, :, :LANE], half_turn(obj[1, :, :LANE]))
    right[...] = jnp.where(low, half_turn(obj[0, :, LANE:]), obj[1, :, LANE:])


def rows_kernel(obj, west, east, mid, top, bottom):
    low = lanes()
    for c in range(2):
        x, y = half_turn(obj[c, :, :LANE]), half_turn(obj[c, :, LANE:])
        w = west[...] if c == 0 else half_turn(west[...])
        e = half_turn(east[...]) if c == 0 else east[...]
        for k, part in enumerate((jnp.where(low, w, x), jnp.where(low, x, y), jnp.where(low, y, e))):
            s = slice(k * LANE, (k + 1) * LANE)
            mid[c, :, s] = part
            top[c, :, s] = part[:H]
            bottom[c, :, s] = part[TILE - H:]


def fetch(refs, scratch, sems):
    copies = [pltpu.make_async_copy(r, t, sems.at[k]) for k, (r, t) in enumerate(zip(refs, scratch))]
    for copy in copies:
        copy.start()

    def wait(*which):
        for k in which:
            copies[k].wait()

    return wait


def store(pairs, sems):
    copies = [pltpu.make_async_copy(x, y, sems.at[k]) for k, (x, y) in enumerate(pairs)]
    for copy in copies:
        copy.start()
    return copies


def finish(copies):
    for copy in copies:
        copy.wait()


def frame_kernel(first, *refs):
    count = 7 if first else 14
    arrays, refs = refs[:count], refs[count:]
    if first:
        keep, send, gu, gm, gd, ext, canvas, outs, *inner, sems = refs
        up, mid, down, off, probe, amps, table = inner
    else:
        keep, send, gu, gm, gd, obj, probe_out, ext, canvas, outs, probe, *inner, sems = refs
        up, mid, down, off, cl, cm, cr, dl, dr, probe_in, mine, other, amps, table = inner
    wait = fetch(arrays, inner, sems)
    wait(*range(4 if first else 9))
    o0 = off[0, 0, 0, 0]
    o1 = off[0, 0, 0, 1]
    row = lax.axis_index("row")
    col = lax.axis_index("col")
    core = lax.rem(col, 2)
    rest = lax.rem(o0, 8)
    base = pl.multiple_of(o0 - rest, 8)
    patch = []
    copies = []
    for c in range(2):
        whole = jnp.concatenate([up[c], mid[c], down[c]], axis=0)
        if not first:
            grad = jnp.concatenate([cl[c] + dl[c], cm[c], cr[c] + dr[c]], axis=1)
            i = lax.broadcasted_iota(jnp.int32, (SPAN, SPAN), 0) + (row * TILE - H)
            j = lax.broadcasted_iota(jnp.int32, (SPAN, SPAN), 1) + (col * TILE - H)
            inside = (i >= 0) & (i < lax.axis_size("row") * TILE) & (j >= 0) & (
                j < lax.axis_size("col") * TILE)
            whole = jnp.where(inside, whole - object_step * grad, 0.0)
        ext[c, :SPAN, :] = whole
        ext[c, SPAN:, :] = jnp.zeros((8, SPAN), f32)
        rows = pltpu.roll(ext[c, pl.ds(base, F + 8), :], SPAN - o1, 1)[:, :F]
        patch.append(pltpu.roll(rows, F + 8 - rest, 0)[:F])
    pr, pi = patch
    if first:
        wait(4, 5, 6)
    else:
        wait(*range(9, 14))
        new_probe(core, probe_in, mine, other, probe)
        copies += store(
            ((ext.at[0, H:H + TILE], obj.at[0]), (ext.at[1, H:H + TILE], obj.at[1]),
             (probe, probe_out)), outs.at[6:9])
    right, left = blocks(table)
    wave = jnp.concatenate(
        [
            jnp.concatenate(
                [
                    probe[0, m] * pr - probe[1, m] * pi,
                    probe[0, m] * pi + probe[1, m] * pr,
                ],
                axis=1,
            )
            for m in range(M)
        ],
        axis=0,
    )
    x = product(split(wave), right)
    x = jnp.concatenate(
        [jnp.concatenate([x[m * F:(m + 1) * F, p * F:(p + 1) * F] for m in range(M)], axis=1)
         for p in range(2)], axis=0)
    x = product(left, split(x))
    square = x[:F] * x[:F] + x[F:] * x[F:]
    intensity = square[:, :F] + square[:, F:]
    factor = 1.0 - amps[0, 0, 0] * lax.rsqrt(intensity + 1.0)
    factor = jnp.concatenate([factor, factor], axis=1)
    x = jnp.concatenate([x[:F] * factor, x[F:] * factor], axis=0)
    x = product(right, split(x))
    x = jnp.concatenate(
        [jnp.concatenate([x[p * F:(p + 1) * F, m * F:(m + 1) * F] for p in range(2)], axis=1)
         for m in range(M)], axis=0)
    x = product(split(x), left)
    ore = jnp.zeros((F, F), f32)
    oim = jnp.zeros((F, F), f32)
    for m in range(M):
        br, bi = x[m * F:(m + 1) * F, :F], x[m * F:(m + 1) * F, F:]
        qr, qi = probe[0, m], probe[1, m]
        ore = ore + (qr * br + qi * bi)
        oim = oim + (qr * bi - qi * br)
        for p, term in enumerate((pr * br + pi * bi, pr * bi - pi * br)):
            s = slice((p * M + m) * F, (p * M + m + 1) * F)
            keep[s, :] = jnp.where(core == 0, term[:, :LANE], term[:, LANE:])
            send[s, :] = jnp.where(core == 0, term[:, LANE:], term[:, :LANE])
    edge = gu.shape[1]
    for c, value in enumerate((ore, oim)):
        canvas[c] = jnp.zeros((SPAN + 8, SPAN), f32)
        value = jnp.concatenate([value, jnp.zeros((8, F), f32)], axis=0)
        value = pltpu.roll(value, rest, 0)
        value = jnp.concatenate([value, jnp.zeros((F + 8, SPAN - F), f32)], axis=1)
        canvas[c, pl.ds(base, F + 8), :] = pltpu.roll(value, o1, 1)
        copies += store(
            ((canvas.at[c, :edge], gu.at[c]), (canvas.at[c, SPAN - edge:SPAN], gd.at[c]),
             (canvas.at[c, edge:SPAN - edge], gm.at[c])), outs.at[3 * c:3 * c + 3])
    finish(copies)


def new_probe(core, probe, mine, other, out):
    coeff = probe_step / (lax.axis_size("row") * lax.axis_size("col"))
    for q in range(4):
        s = slice(q * F, (q + 1) * F)
        x, y = mine[s, :], other[s, :]
        total = jnp.concatenate(
            [jnp.where(core == 0, x, y), jnp.where(core == 0, y, x)], axis=1)
        out[q // 2, q % 2] = probe[q // 2, q % 2] - coeff * total


def chunk_sum(parts, out):
    rows = out.shape[0]
    total = parts[:rows, :]
    for k in range(1, parts.shape[0] // rows):
        total = total + parts[k * rows:(k + 1) * rows, :]
    out[...] = total


def bands_kernel(parts, gu, gm, gd, ru, rd, total, cl, cm, cr, tl, tm, tr, outs, *inner):
    *inner, sems = inner
    wait = fetch((gu, gm, gd, ru, rd), inner, sems)
    gu, gm, gd, ru, rd = inner
    chunk_sum(parts, total)
    wait(*range(5))
    for c in range(2):
        for k, out in enumerate((tl, tm, tr)):
            s = slice(k * B, (k + 1) * B)
            out[c, :B] = gu[c, :, s] + ru[c, :, s]
            out[c, B:2 * B] = gm[c, :, s]
            out[c, 2 * B:] = gd[c, :, s] + rd[c, :, s]
    finish(store(zip((tl, tm, tr), (cl, cm, cr)), outs))


def last_bands_kernel(parts, gm, ru, rd, total, grad_out, left, right, grad, outs, *inner):
    *inner, sems = inner
    wait = fetch((gm, ru, rd), inner, sems)
    gm, ru, rd = inner
    chunk_sum(parts, total)
    low = lanes()
    wait(*range(3))
    for c in range(2):
        grad[c, :H] = gm[c, :H] + ru[c]
        grad[c, H:TILE - H] = gm[c, H:TILE - H]
        grad[c, TILE - H:] = gm[c, TILE - H:] + rd[c]
    copies = store(((grad, grad_out),), outs)
    left[...] = jnp.where(low, grad[0, :, :LANE], half_turn(grad[1, :, :LANE]))
    right[...] = jnp.where(low, half_turn(grad[0, :, 2 * LANE:]), grad[1, :, 2 * LANE:])
    finish(copies)


def spread_kernel(a, b, c, d, out):
    total = (a[...] + b[...]) + (c[...] + d[...])
    rows = a.shape[0]
    for k in range(out.shape[0] // rows):
        out[k * rows:(k + 1) * rows, :] = total


def last_kernel(obj, grad, probe, west, east, mine, other, out, out_probe, *inner):
    *inner, sems = inner
    wait = fetch((obj, grad, probe), inner, sems)
    obj, grad, probe = inner
    low = lanes()
    wait(*range(3))
    for c in range(2):
        w = half_turn(west[...]) if c == 0 else west[...]
        e = east[...] if c == 0 else half_turn(east[...])
        x = obj[c, :, :LANE] - object_step * (grad[c, :, :LANE] + w)
        y = obj[c, :, LANE:2 * LANE] - object_step * grad[c, :, LANE:2 * LANE]
        z = obj[c, :, 2 * LANE:] - object_step * (grad[c, :, 2 * LANE:] + e)
        x, y, z = half_turn(x), half_turn(y), half_turn(z)
        out[c, :, :LANE] = jnp.where(low, x, y)
        out[c, :, LANE:] = jnp.where(low, y, z)
    new_probe(lax.rem(lax.axis_index("col"), 2), probe, mine, other, out_probe)


VM = pl.BlockSpec(memory_space=pltpu.VMEM)
HBM = pl.BlockSpec(memory_space=pltpu.HBM)


def call(kernel, outs, name, limit=SMALL_LIMIT, specs=(), places=(), scratch=()):
    def run(*args):
        held = list(specs) or [VM] * len(args)
        inner = [
            (pltpu.VMEM if x.dtype != jnp.int32 else pltpu.SMEM)(x.shape, x.dtype)
            for x, s in zip(args, held) if s is HBM
        ]
        if inner:
            inner.append(pltpu.SemaphoreType.DMA((len(inner),)))
        return pl.pallas_call(
            kernel,
            out_shape=[jax.ShapeDtypeStruct(s, f32) for s in outs],
            in_specs=held,
            out_specs=list(places) or [VM] * len(outs),
            scratch_shapes=list(scratch) + inner,
            compiler_params=pltpu.CompilerParams(vmem_limit_bytes=limit),
            name=name,
        )(*args)

    return run


def shift(x, axis, step):
    count = lax.axis_size(axis)
    pairs = [(i, i + step) for i in range(count) if 0 <= i + step < count]
    return lax.ppermute(x, axis, pairs)


def exchange(x, mask):
    return lax.ppermute(x, RC, [(i, i ^ mask) for i in range(256)])


def groups(mask):
    members = [i for i in range(256) if i & ~mask == 0]
    return [[base | i for i in members] for base in range(256) if base & mask == 0]


WIDE = BIT_Y | BIT_ZLO | BIT_X
COUNT = 32
CHUNK = 1024 // COUNT


def scatter(keep, send):
    x = keep + exchange(send, BIT_CORE)
    return lax.all_to_all(x, RC, 0, 0, axis_index_groups=groups(WIDE), tiled=True)


def gather(x, *early):
    parts = (x, exchange(x, 2), exchange(x, 4), exchange(x, 6))
    (x,) = call(spread_kernel, [(1024, LANE)], "spread")(*parts)
    x = lax.all_to_all(x, RC, 0, 0, axis_index_groups=groups(WIDE), tiled=True)
    x, *early = lax.optimization_barrier((x, *early))
    return x, exchange(x, BIT_CORE), *early


def local(object_field, probe, amplitudes, offsets):
    table = tables()
    left, right = call(sides_kernel, [(TILE, LANE)] * 2, "sides")(object_field)
    west = shift(right, "col", 1)
    east = shift(left, "col", -1)
    mid, top, bottom = call(
        rows_kernel, [(2, TILE, SPAN)] + [(2, H, SPAN)] * 2, "rows"
    )(object_field, west, east)
    up = shift(bottom, "row", 1)
    down = shift(top, "row", -1)

    halves = [(1024, LANE)] * 2
    canvases = [pltpu.VMEM((2, SPAN + 8, SPAN), f32)] * 2
    keep, send, gu, gm, gd = call(
        functools.partial(frame_kernel, True),
        halves + [(2, B, SPAN)] * 3,
        "frame1",
        VMEM_LIMIT,
        [HBM] * 7,
        [VM] * 2 + [HBM] * 3,
        canvases + [pltpu.SemaphoreType.DMA((6,))],
    )(up, mid, down, offsets, probe, amplitudes, table)
    ru = shift(gd, "row", 1)
    rd = shift(gu, "row", -1)
    total, cl, cm, cr = call(
        bands_kernel,
        [(CHUNK, LANE)] + [(2, SPAN, B)] * 3,
        "bands",
        specs=[VM] + [HBM] * 5,
        places=[VM] + [HBM] * 3,
        scratch=[pltpu.VMEM((2, SPAN, B), f32)] * 3 + [pltpu.SemaphoreType.DMA((3,))],
    )(scatter(keep, send), gu, gm, gd, ru, rd)
    dl = shift(cr, "col", 1)
    dr = shift(cl, "col", -1)
    mine, other, dl, dr = gather(total, dl, dr)

    keep, send, gu, gm, gd, obj, probe = call(
        functools.partial(frame_kernel, False),
        halves + [(2, H, SPAN), (2, TILE, SPAN), (2, H, SPAN), (2, TILE, SPAN), (2, M, F, F)],
        "frame2",
        VMEM_LIMIT,
        [HBM] * 14,
        [VM] * 2 + [HBM] * 5,
        canvases + [pltpu.SemaphoreType.DMA((9,)), pltpu.VMEM((2, M, F, F), f32)],
    )(up, mid, down, offsets, cl, cm, cr, dl, dr, probe, mine, other, amplitudes, table)
    ru = shift(gd, "row", 1)
    rd = shift(gu, "row", -1)
    total, grad, left, right = call(
        last_bands_kernel,
        [(CHUNK, LANE), (2, TILE, SPAN)] + [(TILE, LANE)] * 2,
        "last_bands",
        specs=[VM] + [HBM] * 3,
        places=[VM, HBM, VM, VM],
        scratch=[pltpu.VMEM((2, TILE, SPAN), f32), pltpu.SemaphoreType.DMA((1,))],
    )(scatter(keep, send), gm, ru, rd)
    west = shift(right, "col", 1)
    east = shift(left, "col", -1)
    mine, other, west, east = gather(total, west, east)
    return tuple(
        call(
            last_kernel,
            [(2, TILE, TILE), (2, M, F, F)],
            "last",
            specs=[HBM] * 3 + [VM] * 4,
        )(obj, grad, probe, west, east, mine, other)
    )


def solution(mesh):
    return jax.shard_map(
        local,
        mesh=mesh,
        in_specs=(
            P(None, "row", "col"),
            P(),
            P("row", "col", None, None, None),
            P("row", "col", None, None),
        ),
        out_specs=(P(None, "row", "col"), P()),
        check_vma=False,
    )
```

```python
import functools
import math

import jax
import jax.numpy as jnp
import ml_dtypes
import numpy as np
from jax import lax
from jax.experimental import pallas as pl
from jax.experimental.pallas import tpu as pltpu
from jax.sharding import PartitionSpec as P

H = 64
F = 256
M = 2
TILE = 256
SPAN = TILE + 2 * H
B = 2 * H
object_step = 0.25
probe_step = 4.0
RC = ("row", "col")
BIT_Y, BIT_ZLO, BIT_X, BIT_ZHI, BIT_CORE = 192, 32, 24, 6, 1

f32 = jnp.float32
bf16 = jnp.bfloat16
VMEM_LIMIT = 56 * 1024 * 1024
SMALL_LIMIT = 24 * 1024 * 1024


def tables():
    counter = np.arange(F)
    angle = -2.0 * math.pi / F * (counter[:, None] * counter[None, :] % F)
    out = []
    for table in (np.cos(angle) / math.sqrt(F), np.sin(angle) / math.sqrt(F)):
        high = table.astype(np.float32).astype(ml_dtypes.bfloat16)
        low = (table - high.astype(np.float64)).astype(np.float32).astype(ml_dtypes.bfloat16)
        out += [high, low]
    return np.concatenate(out, axis=0)


def blocks(table):
    rh, rl, ih, il = (table[k * F:(k + 1) * F, :] for k in range(4))

    def block(re, im, under):
        return jnp.concatenate(
            [jnp.concatenate([re, im], axis=1), jnp.concatenate([under, re], axis=1)], axis=0)

    return (block(rh, ih, -ih), block(rl, il, -il)), (block(rh, -ih, ih), block(rl, -il, il))


def split(x):
    high = x.astype(bf16)
    return high, (x - high.astype(f32)).astype(bf16)


def dot(a, b):
    return jnp.dot(a, b, preferred_element_type=f32)


def product(left, right):
    return dot(left[0], right[0]) + (dot(left[0], right[1]) + dot(left[1], right[0]))


LANE = 128


def lanes():
    return lax.broadcasted_iota(jnp.int32, (TILE, LANE), 1) < H


def half_turn(x):
    return pltpu.roll(x, H, 1)


def sides_kernel(obj, left, right):
    low = lanes()
    left[...] = jnp.where(low, obj[0, :, :LANE], half_turn(obj[1, :, :LANE]))
    right[...] = jnp.where(low, half_turn(obj[0, :, LANE:]), obj[1, :, LANE:])


def rows_kernel(obj, west, east, mid, top, bottom):
    low = lanes()
    for c in range(2):
        x, y = half_turn(obj[c, :, :LANE]), half_turn(obj[c, :, LANE:])
        w = west[...] if c == 0 else half_turn(west[...])
        e = half_turn(east[...]) if c == 0 else east[...]
        for k, part in enumerate((jnp.where(low, w, x), jnp.where(low, x, y), jnp.where(low, y, e))):
            s = slice(k * LANE, (k + 1) * LANE)
            mid[c, :, s] = part
            top[c, :, s] = part[:H]
            bottom[c, :, s] = part[TILE - H:]


def fetch(refs, scratch, sems):
    copies = [pltpu.make_async_copy(r, t, sems.at[k]) for k, (r, t) in enumerate(zip(refs, scratch))]
    for copy in copies:
        copy.start()

    def wait(*which):
        for k in which:
            copies[k].wait()

    return wait


def store(pairs, sems):
    copies = [pltpu.make_async_copy(x, y, sems.at[k]) for k, (x, y) in enumerate(pairs)]
    for copy in copies:
        copy.start()
    return copies


def finish(copies):
    for copy in copies:
        copy.wait()


def frame_kernel(first, *refs):
    count = 7 if first else 14
    arrays, refs = refs[:count], refs[count:]
    if first:
        *stores, su, sd, own = refs[:5]
        ext, canvas, raw, head, keep, send, outs, *inner, sems = refs[5:]
        up, mid, down, off, probe, amps, table = inner
    else:
        *stores, su, sd, own, obj, probe_out = refs[:7]
        ext, canvas, raw, head, keep, send, outs, probe, *inner, sems = refs[7:]
        up, mid, down, off, cl, cm, cr, dl, dr, probe_in, mine, other, amps, table = inner
    wait = fetch(arrays, inner, sems)
    wait(*range(4 if first else 9))
    o0 = off[0, 0, 0, 0]
    o1 = off[0, 0, 0, 1]
    row = lax.axis_index("row")
    col = lax.axis_index("col")
    core = lax.rem(col, 2)
    rest = lax.rem(o0, 8)
    base = pl.multiple_of(o0 - rest, 8)
    patch = []
    copies = []
    for c in range(2):
        whole = jnp.concatenate([up[c], mid[c], down[c]], axis=0)
        if not first:
            grad = jnp.concatenate([cl[c] + dl[c], cm[c], cr[c] + dr[c]], axis=1)
            i = lax.broadcasted_iota(jnp.int32, (SPAN, SPAN), 0) + (row * TILE - H)
            j = lax.broadcasted_iota(jnp.int32, (SPAN, SPAN), 1) + (col * TILE - H)
            inside = (i >= 0) & (i < lax.axis_size("row") * TILE) & (j >= 0) & (
                j < lax.axis_size("col") * TILE)
            whole = jnp.where(inside, whole - object_step * grad, 0.0)
        ext[c, :SPAN, :] = whole
        ext[c, SPAN:, :] = jnp.zeros((8, SPAN), f32)
        rows = pltpu.roll(ext[c, pl.ds(base, F + 8), :], SPAN - o1, 1)[:, :F]
        patch.append(pltpu.roll(rows, F + 8 - rest, 0)[:F])
    pr, pi = patch
    if first:
        wait(4, 5, 6)
    else:
        wait(*range(9, 14))
        new_probe(core, probe_in, mine, other, probe)
        copies += store(
            ((ext.at[0, H:H + TILE], obj.at[0]), (ext.at[1, H:H + TILE], obj.at[1]),
             (probe, probe_out)), outs.at[10:13])
    right, left = blocks(table)
    wave = jnp.concatenate(
        [
            jnp.concatenate(
                [
                    probe[0, m] * pr - probe[1, m] * pi,
                    probe[0, m] * pi + probe[1, m] * pr,
                ],
                axis=1,
            )
            for m in range(M)
        ],
        axis=0,
    )
    x = product(split(wave), right)
    x = jnp.concatenate(
        [jnp.concatenate([x[m * F:(m + 1) * F, p * F:(p + 1) * F] for m in range(M)], axis=1)
         for p in range(2)], axis=0)
    x = product(left, split(x))
    square = x[:F] * x[:F] + x[F:] * x[F:]
    intensity = square[:, :F] + square[:, F:]
    factor = 1.0 - amps[0, 0, 0] * lax.rsqrt(intensity + 1.0)
    factor = jnp.concatenate([factor, factor], axis=1)
    x = jnp.concatenate([x[:F] * factor, x[F:] * factor], axis=0)
    x = product(right, split(x))
    x = jnp.concatenate(
        [jnp.concatenate([x[p * F:(p + 1) * F, m * F:(m + 1) * F] for p in range(2)], axis=1)
         for m in range(M)], axis=0)
    x = product(split(x), left)
    ore = jnp.zeros((F, F), f32)
    oim = jnp.zeros((F, F), f32)
    for m in range(M):
        br, bi = x[m * F:(m + 1) * F, :F], x[m * F:(m + 1) * F, F:]
        qr, qi = probe[0, m], probe[1, m]
        ore = ore + (qr * br + qi * bi)
        oim = oim + (qr * bi - qi * br)
        for p, term in enumerate((pr * br + pi * bi, pr * bi - pi * br)):
            s = slice((p * M + m) * F, (p * M + m + 1) * F)
            keep[s, :] = jnp.where(core == 0, term[:, :LANE], term[:, LANE:])
            send[s, :] = jnp.where(core == 0, term[:, LANE:], term[:, :LANE])
    copies += store(zip((keep, send), stores), outs.at[8:10])
    edge = (su.shape[0] - 8) // 2
    skip = (SPAN - own.shape[1]) // 2
    head[...] = jnp.full((8, F), o1.astype(f32))
    for c, value in enumerate((ore, oim)):
        canvas[c] = jnp.zeros((SPAN + 8, SPAN), f32)
        raw[c] = jnp.zeros((SPAN + 8, F), f32)
        value = jnp.concatenate([value, jnp.zeros((8, F), f32)], axis=0)
        value = pltpu.roll(value, rest, 0)
        raw[c, pl.ds(base, F + 8), :] = value
        s = slice(c * edge, (c + 1) * edge)
        copies += store(
            ((raw.at[c, :edge], su.at[s]), (raw.at[c, SPAN - edge:SPAN], sd.at[s])),
            outs.at[2 * c:2 * c + 2])
        canvas[c, pl.ds(base, F + 8), :] = shifted(value, o1)
        copies += store(((canvas.at[c, skip:SPAN - skip], own.at[c]),), outs.at[4 + c:5 + c])
    copies += store(((head, su.at[2 * edge:]), (head, sd.at[2 * edge:])), outs.at[6:8])
    finish(copies)


def shifted(value, columns):
    value = jnp.concatenate([value, jnp.zeros((value.shape[0], SPAN - F), f32)], axis=1)
    return pltpu.roll(value, columns, 1)


def arrived(strip, c):
    edge = (strip.shape[0] - 8) // 2
    columns = jnp.max(strip[2 * edge:, :LANE]).astype(jnp.int32)
    return shifted(strip[c * edge:(c + 1) * edge, :], columns)


def new_probe(core, probe, mine, other, out):
    coeff = probe_step / (lax.axis_size("row") * lax.axis_size("col"))
    for q in range(4):
        s = slice(q * F, (q + 1) * F)
        x, y = mine[s, :], other[s, :]
        total = jnp.concatenate(
            [jnp.where(core == 0, x, y), jnp.where(core == 0, y, x)], axis=1)
        out[q // 2, q % 2] = probe[q // 2, q % 2] - coeff * total


def chunk_sum(parts, out):
    rows = out.shape[0]
    total = parts[:rows, :]
    for k in range(1, parts.shape[0] // rows):
        total = total + parts[k * rows:(k + 1) * rows, :]
    out[...] = total


def bands_kernel(parts, own, ru, rd, total, cl, cm, cr, tl, tm, tr, outs, *inner):
    *inner, sems = inner
    wait = fetch((own, ru, rd), inner, sems)
    own, ru, rd = inner
    chunk_sum(parts, total)
    wait(*range(3))
    for c in range(2):
        above, below = arrived(ru, c), arrived(rd, c)
        for k, out in enumerate((tl, tm, tr)):
            s = slice(k * B, (k + 1) * B)
            out[c, :B] = own[c, :B, s] + above[:, s]
            out[c, B:2 * B] = own[c, B:2 * B, s]
            out[c, 2 * B:] = own[c, 2 * B:, s] + below[:, s]
    finish(store(zip((tl, tm, tr), (cl, cm, cr)), outs))


def last_bands_kernel(parts, own, ru, rd, total, grad_out, left, right, grad, outs, *inner):
    *inner, sems = inner
    wait = fetch((own, ru, rd), inner, sems)
    own, ru, rd = inner
    chunk_sum(parts, total)
    low = lanes()
    wait(*range(3))
    for c in range(2):
        grad[c, :H] = own[c, :H] + arrived(ru, c)
        grad[c, H:TILE - H] = own[c, H:TILE - H]
        grad[c, TILE - H:] = own[c, TILE - H:] + arrived(rd, c)
    copies = store(((grad, grad_out),), outs)
    left[...] = jnp.where(low, grad[0, :, :LANE], half_turn(grad[1, :, :LANE]))
    right[...] = jnp.where(low, half_turn(grad[0, :, 2 * LANE:]), grad[1, :, 2 * LANE:])
    finish(copies)


def spread_kernel(a, b, c, d, out):
    total = (a[...] + b[...]) + (c[...] + d[...])
    rows = a.shape[0]
    for k in range(out.shape[0] // rows):
        out[k * rows:(k + 1) * rows, :] = total


def last_kernel(obj, grad, probe, west, east, mine, other, out, out_probe, *inner):
    *inner, sems = inner
    wait = fetch((obj, grad, probe), inner, sems)
    obj, grad, probe = inner
    low = lanes()
    wait(*range(3))
    for c in range(2):
        w = half_turn(west[...]) if c == 0 else west[...]
        e = east[...] if c == 0 else half_turn(east[...])
        x = obj[c, :, :LANE] - object_step * (grad[c, :, :LANE] + w)
        y = obj[c, :, LANE:2 * LANE] - object_step * grad[c, :, LANE:2 * LANE]
        z = obj[c, :, 2 * LANE:] - object_step * (grad[c, :, 2 * LANE:] + e)
        x, y, z = half_turn(x), half_turn(y), half_turn(z)
        out[c, :, :LANE] = jnp.where(low, x, y)
        out[c, :, LANE:] = jnp.where(low, y, z)
    new_probe(lax.rem(lax.axis_index("col"), 2), probe, mine, other, out_probe)


VM = pl.BlockSpec(memory_space=pltpu.VMEM)
HBM = pl.BlockSpec(memory_space=pltpu.HBM)


def call(kernel, outs, name, limit=SMALL_LIMIT, specs=(), places=(), scratch=()):
    def run(*args):
        held = list(specs) or [VM] * len(args)
        inner = [
            (pltpu.VMEM if x.dtype != jnp.int32 else pltpu.SMEM)(x.shape, x.dtype)
            for x, s in zip(args, held) if s is HBM
        ]
        if inner:
            inner.append(pltpu.SemaphoreType.DMA((len(inner),)))
        return pl.pallas_call(
            kernel,
            out_shape=[jax.ShapeDtypeStruct(s, f32) for s in outs],
            in_specs=held,
            out_specs=list(places) or [VM] * len(outs),
            scratch_shapes=list(scratch) + inner,
            compiler_params=pltpu.CompilerParams(vmem_limit_bytes=limit),
            name=name,
        )(*args)

    return run


def shift(x, axis, step):
    count = lax.axis_size(axis)
    pairs = [(i, i + step) for i in range(count) if 0 <= i + step < count]
    return lax.ppermute(x, axis, pairs)


def exchange(x, mask):
    return lax.ppermute(x, RC, [(i, i ^ mask) for i in range(256)])


def groups(mask):
    members = [i for i in range(256) if i & ~mask == 0]
    return [[base | i for i in members] for base in range(256) if base & mask == 0]


WIDE = BIT_Y | BIT_ZLO | BIT_X
COUNT = 32
CHUNK = 1024 // COUNT


def scatter(keep, send):
    x = keep + exchange(send, BIT_CORE)
    return lax.all_to_all(x, RC, 0, 0, axis_index_groups=groups(WIDE), tiled=True)


def gather(x, *early):
    parts = (x, exchange(x, 2), exchange(x, 4), exchange(x, 6))
    parts, early = lax.optimization_barrier((parts, early))
    (x,) = call(spread_kernel, [(1024, LANE)], "spread")(*parts)
    x = lax.all_to_all(x, RC, 0, 0, axis_index_groups=groups(WIDE), tiled=True)
    return x, exchange(x, BIT_CORE), *early


def local(object_field, probe, amplitudes, offsets):
    table = tables()
    left, right = call(sides_kernel, [(TILE, LANE)] * 2, "sides")(object_field)
    west = shift(right, "col", 1)
    east = shift(left, "col", -1)
    mid, top, bottom = call(
        rows_kernel, [(2, TILE, SPAN)] + [(2, H, SPAN)] * 2, "rows"
    )(object_field, west, east)
    up = shift(bottom, "row", 1)
    down = shift(top, "row", -1)

    halves = [(1024, LANE)] * 2
    held = [pltpu.VMEM((2, SPAN + 8, SPAN), f32)] * 2 + [pltpu.VMEM((2, SPAN + 8, F), f32)]
    held += [pltpu.VMEM((8, F), f32)] + [pltpu.VMEM((1024, LANE), f32)] * 2
    keep, send, su, sd, own = call(
        functools.partial(frame_kernel, True),
        halves + [(2 * B + 8, F)] * 2 + [(2, SPAN, SPAN)],
        "frame1",
        VMEM_LIMIT,
        [HBM] * 7,
        [HBM] * 5,
        held + [pltpu.SemaphoreType.DMA((10,))],
    )(up, mid, down, offsets, probe, amplitudes, table)
    ru = shift(sd, "row", 1)
    rd = shift(su, "row", -1)
    total, cl, cm, cr = call(
        bands_kernel,
        [(CHUNK, LANE)] + [(2, SPAN, B)] * 3,
        "bands",
        specs=[VM] + [HBM] * 3,
        places=[VM] + [HBM] * 3,
        scratch=[pltpu.VMEM((2, SPAN, B), f32)] * 3 + [pltpu.SemaphoreType.DMA((3,))],
    )(scatter(keep, send), own, ru, rd)
    dl = shift(cr, "col", 1)
    dr = shift(cl, "col", -1)
    mine, other, dl, dr = gather(total, dl, dr)

    keep, send, su, sd, own, obj, probe = call(
        functools.partial(frame_kernel, False),
        halves + [(2 * H + 8, F)] * 2 + [(2, TILE, SPAN)] * 2 + [(2, M, F, F)],
        "frame2",
        VMEM_LIMIT,
        [HBM] * 14,
        [HBM] * 7,
        held + [pltpu.SemaphoreType.DMA((13,)), pltpu.VMEM((2, M, F, F), f32)],
    )(up, mid, down, offsets, cl, cm, cr, dl, dr, probe, mine, other, amplitudes, table)
    ru = shift(sd, "row", 1)
    rd = shift(su, "row", -1)
    total, grad, left, right = call(
        last_bands_kernel,
        [(CHUNK, LANE), (2, TILE, SPAN)] + [(TILE, LANE)] * 2,
        "last_bands",
        specs=[VM] + [HBM] * 3,
        places=[VM, HBM, VM, VM],
        scratch=[pltpu.VMEM((2, TILE, SPAN), f32), pltpu.SemaphoreType.DMA((1,))],
    )(scatter(keep, send), own, ru, rd)
    west = shift(right, "col", 1)
    east = shift(left, "col", -1)
    mine, other, west, east = gather(total, west, east)
    return tuple(
        call(
            last_kernel,
            [(2, TILE, TILE), (2, M, F, F)],
            "last",
            specs=[HBM] * 3 + [VM] * 4,
        )(obj, grad, probe, west, east, mine, other)
    )


def solution(mesh):
    return jax.shard_map(
        local,
        mesh=mesh,
        in_specs=(
            P(None, "row", "col"),
            P(),
            P("row", "col", None, None, None),
            P("row", "col", None, None),
        ),
        out_specs=(P(None, "row", "col"), P()),
        check_vma=False,
    )
```

```python
import functools
import math

import jax
import jax.numpy as jnp
import ml_dtypes
import numpy as np
from jax import lax
from jax.experimental import pallas as pl
from jax.experimental.pallas import tpu as pltpu
from jax.sharding import PartitionSpec as P

H = 64
F = 256
M = 2
TILE = 256
SPAN = TILE + 2 * H
B = 2 * H
object_step = 0.25
probe_step = 4.0
RC = ("row", "col")
BIT_Y, BIT_ZLO, BIT_X, BIT_ZHI, BIT_CORE = 192, 32, 24, 6, 1

f32 = jnp.float32
bf16 = jnp.bfloat16
VMEM_LIMIT = 56 * 1024 * 1024
SMALL_LIMIT = 24 * 1024 * 1024


def tables():
    counter = np.arange(F)
    angle = -2.0 * math.pi / F * (counter[:, None] * counter[None, :] % F)
    out = []
    for table in (np.cos(angle) / math.sqrt(F), np.sin(angle) / math.sqrt(F)):
        high = table.astype(np.float32).astype(ml_dtypes.bfloat16)
        low = (table - high.astype(np.float64)).astype(np.float32).astype(ml_dtypes.bfloat16)
        out += [high, low]
    return np.concatenate(out, axis=0)


def blocks(table):
    rh, rl, ih, il = (table[k * F:(k + 1) * F, :] for k in range(4))

    def block(re, im, under):
        return jnp.concatenate(
            [jnp.concatenate([re, im], axis=1), jnp.concatenate([under, re], axis=1)], axis=0)

    return (block(rh, ih, -ih), block(rl, il, -il)), (block(rh, -ih, ih), block(rl, -il, il))


def split(x):
    high = x.astype(bf16)
    return high, (x - high.astype(f32)).astype(bf16)


def dot(a, b):
    return jnp.dot(a, b, preferred_element_type=f32)


def product(left, right):
    return dot(left[0], right[0]) + (dot(left[0], right[1]) + dot(left[1], right[0]))


LANE = 128


def lanes():
    return lax.broadcasted_iota(jnp.int32, (TILE, LANE), 1) < H


def half_turn(x):
    return pltpu.roll(x, H, 1)


def sides_kernel(obj, left, right):
    low = lanes()
    left[...] = jnp.where(low, obj[0, :, :LANE], half_turn(obj[1, :, :LANE]))
    right[...] = jnp.where(low, half_turn(obj[0, :, LANE:]), obj[1, :, LANE:])


def rows_kernel(obj, west, east, mid, top, bottom):
    low = lanes()
    for c in range(2):
        x, y = half_turn(obj[c, :, :LANE]), half_turn(obj[c, :, LANE:])
        w = west[...] if c == 0 else half_turn(west[...])
        e = half_turn(east[...]) if c == 0 else east[...]
        for k, part in enumerate((jnp.where(low, w, x), jnp.where(low, x, y), jnp.where(low, y, e))):
            s = slice(k * LANE, (k + 1) * LANE)
            mid[c, :, s] = part
            top[c, :, s] = part[:H]
            bottom[c, :, s] = part[TILE - H:]


def fetch(refs, scratch, sems):
    copies = [pltpu.make_async_copy(r, t, sems.at[k]) for k, (r, t) in enumerate(zip(refs, scratch))]
    for copy in copies:
        copy.start()

    def wait(*which):
        for k in which:
            copies[k].wait()

    return wait


def store(pairs, sems):
    copies = [pltpu.make_async_copy(x, y, sems.at[k]) for k, (x, y) in enumerate(pairs)]
    for copy in copies:
        copy.start()
    return copies


def finish(copies):
    for copy in copies:
        copy.wait()


def frame_kernel(first, *refs):
    count = 7 if first else 14
    arrays, refs = refs[:count], refs[count:]
    if first:
        *stores, su, sd, own = refs[:5]
        ext, canvas, raw, head, keep, send, outs, *inner, sems = refs[5:]
        up, mid, down, off, probe, amps, table = inner
    else:
        *stores, su, sd, own, obj, probe_out = refs[:7]
        ext, canvas, raw, head, keep, send, outs, probe, *inner, sems = refs[7:]
        up, mid, down, off, cl, cm, cr, dl, dr, probe_in, mine, other, amps, table = inner
    wait = fetch(arrays, inner, sems)
    wait(*range(4 if first else 9))
    o0 = off[0, 0, 0, 0]
    o1 = off[0, 0, 0, 1]
    row = lax.axis_index("row")
    col = lax.axis_index("col")
    core = lax.rem(col, 2)
    rest = lax.rem(o0, 8)
    base = pl.multiple_of(o0 - rest, 8)
    patch = []
    copies = []
    for c in range(2):
        whole = jnp.concatenate([up[c], mid[c], down[c]], axis=0)
        if not first:
            grad = jnp.concatenate([cl[c] + dl[c], cm[c], cr[c] + dr[c]], axis=1)
            i = lax.broadcasted_iota(jnp.int32, (SPAN, SPAN), 0) + (row * TILE - H)
            j = lax.broadcasted_iota(jnp.int32, (SPAN, SPAN), 1) + (col * TILE - H)
            inside = (i >= 0) & (i < lax.axis_size("row") * TILE) & (j >= 0) & (
                j < lax.axis_size("col") * TILE)
            whole = jnp.where(inside, whole - object_step * grad, 0.0)
        ext[c, :SPAN, :] = whole
        ext[c, SPAN:, :] = jnp.zeros((8, SPAN), f32)
        rows = pltpu.roll(ext[c, pl.ds(base, F + 8), :], SPAN - o1, 1)[:, :F]
        patch.append(pltpu.roll(rows, F + 8 - rest, 0)[:F])
    pr, pi = patch
    if first:
        wait(4, 5, 6)
    else:
        wait(*range(9, 14))
        new_probe(core, probe_in, mine, other, probe)
        copies += store(
            ((ext.at[0, H:H + TILE], obj.at[0]), (ext.at[1, H:H + TILE], obj.at[1]),
             (probe, probe_out)), outs.at[10:13])
    right, left = blocks(table)
    wave = jnp.concatenate(
        [
            jnp.concatenate(
                [
                    probe[0, m] * pr - probe[1, m] * pi,
                    probe[0, m] * pi + probe[1, m] * pr,
                ],
                axis=1,
            )
            for m in range(M)
        ],
        axis=0,
    )
    x = product(split(wave), right)
    x = jnp.concatenate(
        [jnp.concatenate([x[m * F:(m + 1) * F, p * F:(p + 1) * F] for m in range(M)], axis=1)
         for p in range(2)], axis=0)
    x = product(left, split(x))
    square = x[:F] * x[:F] + x[F:] * x[F:]
    intensity = square[:, :F] + square[:, F:]
    factor = 1.0 - amps[0, 0, 0] * lax.rsqrt(intensity + 1.0)
    factor = jnp.concatenate([factor, factor], axis=1)
    x = jnp.concatenate([x[:F] * factor, x[F:] * factor], axis=0)
    x = product(right, split(x))
    x = jnp.concatenate(
        [jnp.concatenate([x[p * F:(p + 1) * F, m * F:(m + 1) * F] for p in range(2)], axis=1)
         for m in range(M)], axis=0)
    x = product(split(x), left)
    ore = jnp.zeros((F, F), f32)
    oim = jnp.zeros((F, F), f32)
    for m in range(M):
        br, bi = x[m * F:(m + 1) * F, :F], x[m * F:(m + 1) * F, F:]
        qr, qi = probe[0, m], probe[1, m]
        ore = ore + (qr * br + qi * bi)
        oim = oim + (qr * bi - qi * br)
        for p, term in enumerate((pr * br + pi * bi, pr * bi - pi * br)):
            s = slice((p * M + m) * F, (p * M + m + 1) * F)
            keep[s, :] = jnp.where(core == 0, term[:, :LANE], term[:, LANE:])
            send[s, :] = jnp.where(core == 0, term[:, LANE:], term[:, :LANE])
    copies += store(zip((keep, send), stores), outs.at[8:10])
    edge = (su.shape[0] - 8) // 2
    skip = (SPAN - own.shape[1]) // 2
    head[...] = jnp.full((8, F), o1.astype(f32))
    for c, value in enumerate((ore, oim)):
        canvas[c] = jnp.zeros((SPAN + 8, SPAN), f32)
        raw[c] = jnp.zeros((SPAN + 8, F), f32)
        value = jnp.concatenate([value, jnp.zeros((8, F), f32)], axis=0)
        value = pltpu.roll(value, rest, 0)
        raw[c, pl.ds(base, F + 8), :] = value
        s = slice(c * edge, (c + 1) * edge)
        copies += store(
            ((raw.at[c, :edge], su.at[s]), (raw.at[c, SPAN - edge:SPAN], sd.at[s])),
            outs.at[2 * c:2 * c + 2])
        canvas[c, pl.ds(base, F + 8), :] = shifted(value, o1)
        copies += store(((canvas.at[c, skip:SPAN - skip], own.at[c]),), outs.at[4 + c:5 + c])
    copies += store(((head, su.at[2 * edge:]), (head, sd.at[2 * edge:])), outs.at[6:8])
    finish(copies)


def shifted(value, columns):
    value = jnp.concatenate([value, jnp.zeros((value.shape[0], SPAN - F), f32)], axis=1)
    return pltpu.roll(value, columns, 1)


def arrived(strip, c):
    edge = (strip.shape[0] - 8) // 2
    columns = jnp.max(strip[2 * edge:, :LANE]).astype(jnp.int32)
    return shifted(strip[c * edge:(c + 1) * edge, :], columns)


def new_probe(core, probe, mine, other, out):
    coeff = probe_step / (lax.axis_size("row") * lax.axis_size("col"))
    for q in range(4):
        s = slice(q * F, (q + 1) * F)
        x, y = mine[s, :], other[s, :]
        total = jnp.concatenate(
            [jnp.where(core == 0, x, y), jnp.where(core == 0, y, x)], axis=1)
        out[q // 2, q % 2] = probe[q // 2, q % 2] - coeff * total


def bands_kernel(keep, recv, own, ru, rd, half, cl, cm, cr, th, tl, tm, tr, outs, *inner):
    *inner, sems = inner
    wait = fetch((keep, recv, own, ru, rd), inner, sems)
    keep, recv, own, ru, rd = inner
    wait(0, 1)
    th[...] = keep[...] + recv[...]
    copies = store(((th, half),), outs)
    wait(2, 3, 4)
    for c in range(2):
        above, below = arrived(ru, c), arrived(rd, c)
        for k, out in enumerate((tl, tm, tr)):
            s = slice(k * B, (k + 1) * B)
            out[c, :B] = own[c, :B, s] + above[:, s]
            out[c, B:2 * B] = own[c, B:2 * B, s]
            out[c, 2 * B:] = own[c, 2 * B:, s] + below[:, s]
    finish(copies + store(zip((tl, tm, tr), (cl, cm, cr)), outs.at[1:4]))


def last_bands_kernel(keep, recv, own, ru, rd, half, grad_out, left, right, th, grad, outs, *inner):
    *inner, sems = inner
    wait = fetch((keep, recv, own, ru, rd), inner, sems)
    keep, recv, own, ru, rd = inner
    wait(0, 1)
    th[...] = keep[...] + recv[...]
    copies = store(((th, half),), outs)
    low = lanes()
    wait(2, 3, 4)
    for c in range(2):
        grad[c, :H] = own[c, :H] + arrived(ru, c)
        grad[c, H:TILE - H] = own[c, H:TILE - H]
        grad[c, TILE - H:] = own[c, TILE - H:] + arrived(rd, c)
    copies += store(((grad, grad_out),), outs.at[1:2])
    left[...] = jnp.where(low, grad[0, :, :LANE], half_turn(grad[1, :, :LANE]))
    right[...] = jnp.where(low, half_turn(grad[0, :, 2 * LANE:]), grad[1, :, 2 * LANE:])
    finish(copies)


def spread_kernel(a, b, c, d, out):
    total = (a[...] + b[...]) + (c[...] + d[...])
    rows = a.shape[0]
    for k in range(out.shape[0] // rows):
        out[k * rows:(k + 1) * rows, :] = total


def last_kernel(obj, grad, probe, west, east, mine, other, out, out_probe, *inner):
    *inner, sems = inner
    wait = fetch((obj, grad, probe), inner, sems)
    obj, grad, probe = inner
    low = lanes()
    wait(*range(3))
    for c in range(2):
        w = half_turn(west[...]) if c == 0 else west[...]
        e = east[...] if c == 0 else half_turn(east[...])
        x = obj[c, :, :LANE] - object_step * (grad[c, :, :LANE] + w)
        y = obj[c, :, LANE:2 * LANE] - object_step * grad[c, :, LANE:2 * LANE]
        z = obj[c, :, 2 * LANE:] - object_step * (grad[c, :, 2 * LANE:] + e)
        x, y, z = half_turn(x), half_turn(y), half_turn(z)
        out[c, :, :LANE] = jnp.where(low, x, y)
        out[c, :, LANE:] = jnp.where(low, y, z)
    new_probe(lax.rem(lax.axis_index("col"), 2), probe, mine, other, out_probe)


VM = pl.BlockSpec(memory_space=pltpu.VMEM)
HBM = pl.BlockSpec(memory_space=pltpu.HBM)


def call(kernel, outs, name, limit=SMALL_LIMIT, specs=(), places=(), scratch=()):
    def run(*args):
        held = list(specs) or [VM] * len(args)
        inner = [
            (pltpu.VMEM if x.dtype != jnp.int32 else pltpu.SMEM)(x.shape, x.dtype)
            for x, s in zip(args, held) if s is HBM
        ]
        if inner:
            inner.append(pltpu.SemaphoreType.DMA((len(inner),)))
        return pl.pallas_call(
            kernel,
            out_shape=[jax.ShapeDtypeStruct(s, f32) for s in outs],
            in_specs=held,
            out_specs=list(places) or [VM] * len(outs),
            scratch_shapes=list(scratch) + inner,
            compiler_params=pltpu.CompilerParams(vmem_limit_bytes=limit),
            name=name,
        )(*args)

    return run


def shift(x, axis, step):
    count = lax.axis_size(axis)
    pairs = [(i, i + step) for i in range(count) if 0 <= i + step < count]
    return lax.ppermute(x, axis, pairs)


def exchange(x, mask):
    return lax.ppermute(x, RC, [(i, i ^ mask) for i in range(256)])


def groups(mask):
    members = [i for i in range(256) if i & ~mask == 0]
    return [[base | i for i in members] for base in range(256) if base & mask == 0]


WIDE = BIT_Y | BIT_ZLO | BIT_X
COUNT = 32
CHUNK = 1024 // COUNT


def total_of(x, *early):
    x = lax.all_to_all(x, RC, 0, 0, axis_index_groups=groups(WIDE), tiled=True)
    x, early = lax.optimization_barrier((x, early))
    x = x.reshape(COUNT, CHUNK, LANE).sum(axis=0)
    parts = (x, exchange(x, 2), exchange(x, 4), exchange(x, 6))
    (x,) = call(spread_kernel, [(1024, LANE)], "spread")(*parts)
    x = lax.all_to_all(x, RC, 0, 0, axis_index_groups=groups(WIDE), tiled=True)
    return x, exchange(x, BIT_CORE), *early


def local(object_field, probe, amplitudes, offsets):
    table = tables()
    left, right = call(sides_kernel, [(TILE, LANE)] * 2, "sides")(object_field)
    west = shift(right, "col", 1)
    east = shift(left, "col", -1)
    mid, top, bottom = call(
        rows_kernel, [(2, TILE, SPAN)] + [(2, H, SPAN)] * 2, "rows"
    )(object_field, west, east)
    up = shift(bottom, "row", 1)
    down = shift(top, "row", -1)

    halves = [(1024, LANE)] * 2
    held = [pltpu.VMEM((2, SPAN + 8, SPAN), f32)] * 2 + [pltpu.VMEM((2, SPAN + 8, F), f32)]
    held += [pltpu.VMEM((8, F), f32)] + [pltpu.VMEM((1024, LANE), f32)] * 2
    keep, send, su, sd, own = call(
        functools.partial(frame_kernel, True),
        halves + [(2 * B + 8, F)] * 2 + [(2, SPAN, SPAN)],
        "frame1",
        VMEM_LIMIT,
        [HBM] * 7,
        [HBM] * 5,
        held + [pltpu.SemaphoreType.DMA((10,))],
    )(up, mid, down, offsets, probe, amplitudes, table)
    ru = shift(sd, "row", 1)
    rd = shift(su, "row", -1)
    half, cl, cm, cr = call(
        bands_kernel,
        [(1024, LANE)] + [(2, SPAN, B)] * 3,
        "bands",
        VMEM_LIMIT,
        specs=[HBM] * 5,
        places=[HBM] * 4,
        scratch=[pltpu.VMEM((1024, LANE), f32)]
        + [pltpu.VMEM((2, SPAN, B), f32)] * 3
        + [pltpu.SemaphoreType.DMA((4,))],
    )(keep, exchange(send, BIT_CORE), own, ru, rd)
    dl = shift(cr, "col", 1)
    dr = shift(cl, "col", -1)
    mine, other, dl, dr = total_of(half, dl, dr)

    keep, send, su, sd, own, obj, probe = call(
        functools.partial(frame_kernel, False),
        halves + [(2 * H + 8, F)] * 2 + [(2, TILE, SPAN)] * 2 + [(2, M, F, F)],
        "frame2",
        VMEM_LIMIT,
        [HBM] * 14,
        [HBM] * 7,
        held + [pltpu.SemaphoreType.DMA((13,)), pltpu.VMEM((2, M, F, F), f32)],
    )(up, mid, down, offsets, cl, cm, cr, dl, dr, probe, mine, other, amplitudes, table)
    ru = shift(sd, "row", 1)
    rd = shift(su, "row", -1)
    half, grad, left, right = call(
        last_bands_kernel,
        [(1024, LANE), (2, TILE, SPAN)] + [(TILE, LANE)] * 2,
        "last_bands",
        VMEM_LIMIT,
        specs=[HBM] * 5,
        places=[HBM, HBM, VM, VM],
        scratch=[pltpu.VMEM((1024, LANE), f32), pltpu.VMEM((2, TILE, SPAN), f32)]
        + [pltpu.SemaphoreType.DMA((2,))],
    )(keep, exchange(send, BIT_CORE), own, ru, rd)
    west = shift(right, "col", 1)
    east = shift(left, "col", -1)
    mine, other, west, east = total_of(half, west, east)
    return tuple(
        call(
            last_kernel,
            [(2, TILE, TILE), (2, M, F, F)],
            "last",
            specs=[HBM] * 3 + [VM] * 4,
        )(obj, grad, probe, west, east, mine, other)
    )


def solution(mesh):
    return jax.shard_map(
        local,
        mesh=mesh,
        in_specs=(
            P(None, "row", "col"),
            P(),
            P("row", "col", None, None, None),
            P("row", "col", None, None),
        ),
        out_specs=(P(None, "row", "col"), P()),
        check_vma=False,
    )
```

```python
import functools
import math

import jax
import jax.numpy as jnp
import ml_dtypes
import numpy as np
from jax import lax
from jax.experimental import pallas as pl
from jax.experimental.pallas import tpu as pltpu
from jax.sharding import PartitionSpec as P

H = 64
F = 256
M = 2
TILE = 256
SPAN = TILE + 2 * H
B = 2 * H
object_step = 0.25
probe_step = 4.0
RC = ("row", "col")
BIT_Y, BIT_ZLO, BIT_X, BIT_ZHI, BIT_CORE = 192, 32, 24, 6, 1

f32 = jnp.float32
bf16 = jnp.bfloat16
VMEM_LIMIT = 56 * 1024 * 1024
SMALL_LIMIT = 24 * 1024 * 1024


def tables():
    counter = np.arange(F)
    angle = -2.0 * math.pi / F * (counter[:, None] * counter[None, :] % F)
    out = []
    for table in (np.cos(angle) / math.sqrt(F), np.sin(angle) / math.sqrt(F)):
        high = table.astype(np.float32).astype(ml_dtypes.bfloat16)
        low = (table - high.astype(np.float64)).astype(np.float32).astype(ml_dtypes.bfloat16)
        out += [high, low]
    return np.concatenate(out, axis=0)


def blocks(table):
    rh, rl, ih, il = (table[k * F:(k + 1) * F, :] for k in range(4))

    def block(re, im, under):
        return jnp.concatenate(
            [jnp.concatenate([re, im], axis=1), jnp.concatenate([under, re], axis=1)], axis=0)

    return (block(rh, ih, -ih), block(rl, il, -il)), (block(rh, -ih, ih), block(rl, -il, il))


def split(x):
    high = x.astype(bf16)
    return high, (x - high.astype(f32)).astype(bf16)


def dot(a, b):
    return jnp.dot(a, b, preferred_element_type=f32)


def product(left, right):
    return dot(left[0], right[0]) + (dot(left[0], right[1]) + dot(left[1], right[0]))


LANE = 128


def lanes():
    return lax.broadcasted_iota(jnp.int32, (TILE, LANE), 1) < H


def half_turn(x):
    return pltpu.roll(x, H, 1)


def core_index():
    return lax.rem(lax.axis_index("col"), 2)


def choose(x, y):
    return jnp.where(core_index() == 0, x, y)


def sides_kernel(obj, inner, outer):
    low = lanes()
    left = jnp.where(low, obj[0, :, :LANE], half_turn(obj[1, :, :LANE]))
    right = jnp.where(low, half_turn(obj[0, :, LANE:]), obj[1, :, LANE:])
    inner[...] = choose(right, left)
    outer[...] = choose(left, right)


def rows_kernel(obj, inner, outer, mid, top, bottom):
    low = lanes()
    west, east = choose(outer[...], inner[...]), choose(inner[...], outer[...])
    for c in range(2):
        x, y = half_turn(obj[c, :, :LANE]), half_turn(obj[c, :, LANE:])
        w = west if c == 0 else half_turn(west)
        e = half_turn(east) if c == 0 else east
        for k, part in enumerate((jnp.where(low, w, x), jnp.where(low, x, y), jnp.where(low, y, e))):
            s = slice(k * LANE, (k + 1) * LANE)
            mid[c, :, s] = part
            top[c, :, s] = part[:H]
            bottom[c, :, s] = part[TILE - H:]


def fetch(refs, scratch, sems):
    copies = [pltpu.make_async_copy(r, t, sems.at[k]) for k, (r, t) in enumerate(zip(refs, scratch))]
    for copy in copies:
        copy.start()

    def wait(*which):
        for k in which:
            copies[k].wait()

    return wait


def store(pairs, sems):
    copies = [pltpu.make_async_copy(x, y, sems.at[k]) for k, (x, y) in enumerate(pairs)]
    for copy in copies:
        copy.start()
    return copies


def finish(copies):
    for copy in copies:
        copy.wait()


def frame_kernel(first, *refs):
    count = 7 if first else 14
    arrays, refs = refs[:count], refs[count:]
    if first:
        *stores, su, sd, own = refs[:5]
        ext, canvas, raw, head, keep, send, outs, *inner, sems = refs[5:]
        up, mid, down, off, probe, amps, table = inner
    else:
        *stores, su, sd, own, obj, probe_out = refs[:7]
        ext, canvas, raw, head, keep, send, outs, probe, *inner, sems = refs[7:]
        up, mid, down, off, ci, cm, co, di, do, probe_in, mine, other, amps, table = inner
    wait = fetch(arrays, inner, sems)
    wait(*range(4 if first else 9))
    o0 = off[0, 0, 0, 0]
    o1 = off[0, 0, 0, 1]
    row = lax.axis_index("row")
    col = lax.axis_index("col")
    core = lax.rem(col, 2)
    rest = lax.rem(o0, 8)
    base = pl.multiple_of(o0 - rest, 8)
    patch = []
    copies = []
    for c in range(2):
        whole = jnp.concatenate([up[c], mid[c], down[c]], axis=0)
        if not first:
            near, far = ci[c] + di[c], co[c] + do[c]
            grad = jnp.concatenate([choose(far, near), cm[c], choose(near, far)], axis=1)
            i = lax.broadcasted_iota(jnp.int32, (SPAN, SPAN), 0) + (row * TILE - H)
            j = lax.broadcasted_iota(jnp.int32, (SPAN, SPAN), 1) + (col * TILE - H)
            inside = (i >= 0) & (i < lax.axis_size("row") * TILE) & (j >= 0) & (
                j < lax.axis_size("col") * TILE)
            whole = jnp.where(inside, whole - object_step * grad, 0.0)
        ext[c, :SPAN, :] = whole
        ext[c, SPAN:, :] = jnp.zeros((8, SPAN), f32)
        rows = pltpu.roll(ext[c, pl.ds(base, F + 8), :], SPAN - o1, 1)[:, :F]
        patch.append(pltpu.roll(rows, F + 8 - rest, 0)[:F])
    pr, pi = patch
    if first:
        wait(4, 5, 6)
    else:
        wait(*range(9, 14))
        new_probe(core, probe_in, mine, other, probe)
        copies += store(
            ((ext.at[0, H:H + TILE], obj.at[0]), (ext.at[1, H:H + TILE], obj.at[1]),
             (probe, probe_out)), outs.at[10:13])
    right, left = blocks(table)
    wave = jnp.concatenate(
        [
            jnp.concatenate(
                [
                    probe[0, m] * pr - probe[1, m] * pi,
                    probe[0, m] * pi + probe[1, m] * pr,
                ],
                axis=1,
            )
            for m in range(M)
        ],
        axis=0,
    )
    x = product(split(wave), right)
    x = jnp.concatenate(
        [jnp.concatenate([x[m * F:(m + 1) * F, p * F:(p + 1) * F] for m in range(M)], axis=1)
         for p in range(2)], axis=0)
    x = product(left, split(x))
    square = x[:F] * x[:F] + x[F:] * x[F:]
    intensity = square[:, :F] + square[:, F:]
    factor = 1.0 - amps[0, 0, 0] * lax.rsqrt(intensity + 1.0)
    factor = jnp.concatenate([factor, factor], axis=1)
    x = jnp.concatenate([x[:F] * factor, x[F:] * factor], axis=0)
    x = product(right, split(x))
    x = jnp.concatenate(
        [jnp.concatenate([x[p * F:(p + 1) * F, m * F:(m + 1) * F] for p in range(2)], axis=1)
         for m in range(M)], axis=0)
    x = product(split(x), left)
    ore = jnp.zeros((F, F), f32)
    oim = jnp.zeros((F, F), f32)
    for m in range(M):
        br, bi = x[m * F:(m + 1) * F, :F], x[m * F:(m + 1) * F, F:]
        qr, qi = probe[0, m], probe[1, m]
        ore = ore + (qr * br + qi * bi)
        oim = oim + (qr * bi - qi * br)
        for p, term in enumerate((pr * br + pi * bi, pr * bi - pi * br)):
            s = slice((p * M + m) * F, (p * M + m + 1) * F)
            keep[s, :] = jnp.where(core == 0, term[:, :LANE], term[:, LANE:])
            send[s, :] = jnp.where(core == 0, term[:, LANE:], term[:, :LANE])
    copies += store(zip((keep, send), stores), outs.at[8:10])
    edge = (su.shape[0] - 8) // 2
    skip = (SPAN - own.shape[1]) // 2
    head[...] = jnp.full((8, F), o1.astype(f32))
    for c, value in enumerate((ore, oim)):
        canvas[c] = jnp.zeros((SPAN + 8, SPAN), f32)
        raw[c] = jnp.zeros((SPAN + 8, F), f32)
        value = jnp.concatenate([value, jnp.zeros((8, F), f32)], axis=0)
        value = pltpu.roll(value, rest, 0)
        raw[c, pl.ds(base, F + 8), :] = value
        s = slice(c * edge, (c + 1) * edge)
        copies += store(
            ((raw.at[c, :edge], su.at[s]), (raw.at[c, SPAN - edge:SPAN], sd.at[s])),
            outs.at[2 * c:2 * c + 2])
        canvas[c, pl.ds(base, F + 8), :] = shifted(value, o1)
        copies += store(((canvas.at[c, skip:SPAN - skip], own.at[c]),), outs.at[4 + c:5 + c])
    copies += store(((head, su.at[2 * edge:]), (head, sd.at[2 * edge:])), outs.at[6:8])
    finish(copies)


def shifted(value, columns):
    value = jnp.concatenate([value, jnp.zeros((value.shape[0], SPAN - F), f32)], axis=1)
    return pltpu.roll(value, columns, 1)


def arrived(strip, c):
    edge = (strip.shape[0] - 8) // 2
    columns = jnp.max(strip[2 * edge:, :LANE]).astype(jnp.int32)
    return shifted(strip[c * edge:(c + 1) * edge, :], columns)


def new_probe(core, probe, mine, other, out):
    coeff = probe_step / (lax.axis_size("row") * lax.axis_size("col"))
    for q in range(4):
        s = slice(q * F, (q + 1) * F)
        x, y = mine[s, :], other[s, :]
        total = jnp.concatenate(
            [jnp.where(core == 0, x, y), jnp.where(core == 0, y, x)], axis=1)
        out[q // 2, q % 2] = probe[q // 2, q % 2] - coeff * total


def chunk_sum(parts, out):
    rows = out.shape[0]
    total = parts[:rows, :]
    for k in range(1, parts.shape[0] // rows):
        total = total + parts[k * rows:(k + 1) * rows, :]
    out[...] = total


def bands_kernel(parts, own, ru, rd, total, ci, cm, co, ti, tm, to, outs, *inner):
    *inner, sems = inner
    wait = fetch((own, ru, rd), inner, sems)
    own, ru, rd = inner
    chunk_sum(parts, total)
    wait(*range(3))
    for c in range(2):
        rows = jnp.concatenate(
            [own[c, :B] + arrived(ru, c), own[c, B:2 * B], own[c, 2 * B:] + arrived(rd, c)], axis=0)
        left, tm[c], right = rows[:, :B], rows[:, B:2 * B], rows[:, 2 * B:]
        ti[c] = choose(right, left)
        to[c] = choose(left, right)
    finish(store(zip((ti, to, tm), (ci, co, cm)), outs))


def last_bands_kernel(parts, own, ru, rd, total, grad_out, near, far, grad, outs, *inner):
    *inner, sems = inner
    wait = fetch((own, ru, rd), inner, sems)
    own, ru, rd = inner
    chunk_sum(parts, total)
    low = lanes()
    wait(*range(3))
    for c in range(2):
        grad[c, :H] = own[c, :H] + arrived(ru, c)
        grad[c, H:TILE - H] = own[c, H:TILE - H]
        grad[c, TILE - H:] = own[c, TILE - H:] + arrived(rd, c)
    copies = store(((grad, grad_out),), outs)
    left = jnp.where(low, grad[0, :, :LANE], half_turn(grad[1, :, :LANE]))
    right = jnp.where(low, half_turn(grad[0, :, 2 * LANE:]), grad[1, :, 2 * LANE:])
    near[...] = choose(right, left)
    far[...] = choose(left, right)
    finish(copies)


def spread_kernel(a, b, c, d, out):
    total = (a[...] + b[...]) + (c[...] + d[...])
    rows = a.shape[0]
    for k in range(out.shape[0] // rows):
        out[k * rows:(k + 1) * rows, :] = total


def last_kernel(obj, grad, probe, near, far, mine, other, out, out_probe, *inner):
    *inner, sems = inner
    wait = fetch((obj, grad, probe), inner, sems)
    obj, grad, probe = inner
    low = lanes()
    west, east = choose(far[...], near[...]), choose(near[...], far[...])
    wait(*range(3))
    for c in range(2):
        w = half_turn(west) if c == 0 else west
        e = east if c == 0 else half_turn(east)
        x = obj[c, :, :LANE] - object_step * (grad[c, :, :LANE] + w)
        y = obj[c, :, LANE:2 * LANE] - object_step * grad[c, :, LANE:2 * LANE]
        z = obj[c, :, 2 * LANE:] - object_step * (grad[c, :, 2 * LANE:] + e)
        x, y, z = half_turn(x), half_turn(y), half_turn(z)
        out[c, :, :LANE] = jnp.where(low, x, y)
        out[c, :, LANE:] = jnp.where(low, y, z)
    new_probe(lax.rem(lax.axis_index("col"), 2), probe, mine, other, out_probe)


VM = pl.BlockSpec(memory_space=pltpu.VMEM)
HBM = pl.BlockSpec(memory_space=pltpu.HBM)


def call(kernel, outs, name, limit=SMALL_LIMIT, specs=(), places=(), scratch=()):
    def run(*args):
        held = list(specs) or [VM] * len(args)
        inner = [
            (pltpu.VMEM if x.dtype != jnp.int32 else pltpu.SMEM)(x.shape, x.dtype)
            for x, s in zip(args, held) if s is HBM
        ]
        if inner:
            inner.append(pltpu.SemaphoreType.DMA((len(inner),)))
        return pl.pallas_call(
            kernel,
            out_shape=[jax.ShapeDtypeStruct(s, f32) for s in outs],
            in_specs=held,
            out_specs=list(places) or [VM] * len(outs),
            scratch_shapes=list(scratch) + inner,
            compiler_params=pltpu.CompilerParams(vmem_limit_bytes=limit),
            name=name,
        )(*args)

    return run


def shift(x, axis, step):
    count = lax.axis_size(axis)
    pairs = [(i, i + step) for i in range(count) if 0 <= i + step < count]
    return lax.ppermute(x, axis, pairs)


def exchange(x, mask):
    return lax.ppermute(x, RC, [(i, i ^ mask) for i in range(256)])


def columns(near, far):
    count = lax.axis_size("col")
    pairs = [(i, i + 1) for i in range(1, count - 1, 2)]
    pairs += [(j, i) for i, j in pairs]
    return exchange(near, BIT_CORE), lax.ppermute(far, "col", pairs)


def groups(mask):
    members = [i for i in range(256) if i & ~mask == 0]
    return [[base | i for i in members] for base in range(256) if base & mask == 0]


WIDE = BIT_Y | BIT_ZLO | BIT_X
COUNT = 32
CHUNK = 1024 // COUNT


def scatter(keep, send):
    x = keep + exchange(send, BIT_CORE)
    return lax.all_to_all(x, RC, 0, 0, axis_index_groups=groups(WIDE), tiled=True)


def gather(x, *early):
    parts = (x, exchange(x, 2), exchange(x, 4), exchange(x, 6))
    parts, early = lax.optimization_barrier((parts, early))
    (x,) = call(spread_kernel, [(1024, LANE)], "spread")(*parts)
    x = lax.all_to_all(x, RC, 0, 0, axis_index_groups=groups(WIDE), tiled=True)
    return x, exchange(x, BIT_CORE), *early


def local(object_field, probe, amplitudes, offsets):
    table = tables()
    sides = call(sides_kernel, [(TILE, LANE)] * 2, "sides")(object_field)
    mid, top, bottom = call(
        rows_kernel, [(2, TILE, SPAN)] + [(2, H, SPAN)] * 2, "rows"
    )(object_field, *columns(*sides))
    up = shift(bottom, "row", 1)
    down = shift(top, "row", -1)

    halves = [(1024, LANE)] * 2
    held = [pltpu.VMEM((2, SPAN + 8, SPAN), f32)] * 2 + [pltpu.VMEM((2, SPAN + 8, F), f32)]
    held += [pltpu.VMEM((8, F), f32)] + [pltpu.VMEM((1024, LANE), f32)] * 2
    keep, send, su, sd, own = call(
        functools.partial(frame_kernel, True),
        halves + [(2 * B + 8, F)] * 2 + [(2, SPAN, SPAN)],
        "frame1",
        VMEM_LIMIT,
        [HBM] * 7,
        [HBM] * 5,
        held + [pltpu.SemaphoreType.DMA((10,))],
    )(up, mid, down, offsets, probe, amplitudes, table)
    ru = shift(sd, "row", 1)
    rd = shift(su, "row", -1)
    total, ci, cm, co = call(
        bands_kernel,
        [(CHUNK, LANE)] + [(2, SPAN, B)] * 3,
        "bands",
        specs=[VM] + [HBM] * 3,
        places=[VM] + [HBM] * 3,
        scratch=[pltpu.VMEM((2, SPAN, B), f32)] * 3 + [pltpu.SemaphoreType.DMA((3,))],
    )(scatter(keep, send), own, ru, rd)
    mine, other, di, do = gather(total, *columns(ci, co))

    keep, send, su, sd, own, obj, probe = call(
        functools.partial(frame_kernel, False),
        halves + [(2 * H + 8, F)] * 2 + [(2, TILE, SPAN)] * 2 + [(2, M, F, F)],
        "frame2",
        VMEM_LIMIT,
        [HBM] * 14,
        [HBM] * 7,
        held + [pltpu.SemaphoreType.DMA((13,)), pltpu.VMEM((2, M, F, F), f32)],
    )(up, mid, down, offsets, ci, cm, co, di, do, probe, mine, other, amplitudes, table)
    ru = shift(sd, "row", 1)
    rd = shift(su, "row", -1)
    total, grad, near, far = call(
        last_bands_kernel,
        [(CHUNK, LANE), (2, TILE, SPAN)] + [(TILE, LANE)] * 2,
        "last_bands",
        specs=[VM] + [HBM] * 3,
        places=[VM, HBM, VM, VM],
        scratch=[pltpu.VMEM((2, TILE, SPAN), f32), pltpu.SemaphoreType.DMA((1,))],
    )(scatter(keep, send), own, ru, rd)
    mine, other, near, far = gather(total, *columns(near, far))
    return tuple(
        call(
            last_kernel,
            [(2, TILE, TILE), (2, M, F, F)],
            "last",
            specs=[HBM] * 3 + [VM] * 4,
        )(obj, grad, probe, near, far, mine, other)
    )


def solution(mesh):
    return jax.shard_map(
        local,
        mesh=mesh,
        in_specs=(
            P(None, "row", "col"),
            P(),
            P("row", "col", None, None, None),
            P("row", "col", None, None),
        ),
        out_specs=(P(None, "row", "col"), P()),
        check_vma=False,
    )
```

```python
import functools
import math

import jax
import jax.numpy as jnp
import ml_dtypes
import numpy as np
from jax import lax
from jax.experimental import pallas as pl
from jax.experimental.pallas import tpu as pltpu
from jax.sharding import PartitionSpec as P

H = 64
F = 256
M = 2
TILE = 256
SPAN = TILE + 2 * H
B = 2 * H
object_step = 0.25
probe_step = 4.0
RC = ("row", "col")
BIT_Y, BIT_ZLO, BIT_X, BIT_ZHI, BIT_CORE = 192, 32, 24, 6, 1

f32 = jnp.float32
bf16 = jnp.bfloat16
VMEM_LIMIT = 56 * 1024 * 1024
SMALL_LIMIT = 24 * 1024 * 1024


def tables():
    counter = np.arange(F)
    angle = -2.0 * math.pi / F * (counter[:, None] * counter[None, :] % F)
    out = []
    for table in (np.cos(angle) / math.sqrt(F), np.sin(angle) / math.sqrt(F)):
        high = table.astype(np.float32).astype(ml_dtypes.bfloat16)
        low = (table - high.astype(np.float64)).astype(np.float32).astype(ml_dtypes.bfloat16)
        out += [high, low]
    return np.concatenate(out, axis=0)


def blocks(table):
    rh, rl, ih, il = (table[k * F:(k + 1) * F, :] for k in range(4))

    def block(re, im, under):
        return jnp.concatenate(
            [jnp.concatenate([re, im], axis=1), jnp.concatenate([under, re], axis=1)], axis=0)

    return (block(rh, ih, -ih), block(rl, il, -il)), (block(rh, -ih, ih), block(rl, -il, il))


def split(x):
    high = x.astype(bf16)
    return high, (x - high.astype(f32)).astype(bf16)


def dot(a, b):
    return jnp.dot(a, b, preferred_element_type=f32)


def product(left, right):
    return dot(left[0], right[0]) + (dot(left[0], right[1]) + dot(left[1], right[0]))


LANE = 128


def lanes():
    return lax.broadcasted_iota(jnp.int32, (TILE, LANE), 1) < H


def half_turn(x):
    return pltpu.roll(x, H, 1)


def core_index():
    return lax.rem(lax.axis_index("col"), 2)


def choose(x, y):
    return jnp.where(core_index() == 0, x, y)


def sides_kernel(obj, inner, outer):
    low = lanes()
    left = jnp.where(low, obj[0, :, :LANE], half_turn(obj[1, :, :LANE]))
    right = jnp.where(low, half_turn(obj[0, :, LANE:]), obj[1, :, LANE:])
    inner[...] = choose(right, left)
    outer[...] = choose(left, right)


def rows_kernel(obj, inner, outer, mid, top, bottom):
    low = lanes()
    west, east = choose(outer[...], inner[...]), choose(inner[...], outer[...])
    for c in range(2):
        x, y = half_turn(obj[c, :, :LANE]), half_turn(obj[c, :, LANE:])
        w = west if c == 0 else half_turn(west)
        e = half_turn(east) if c == 0 else east
        for k, part in enumerate((jnp.where(low, w, x), jnp.where(low, x, y), jnp.where(low, y, e))):
            s = slice(k * LANE, (k + 1) * LANE)
            mid[c, :, s] = part
            top[c, :, s] = part[:H]
            bottom[c, :, s] = part[TILE - H:]


def fetch(refs, scratch, sems):
    copies = [pltpu.make_async_copy(r, t, sems.at[k]) for k, (r, t) in enumerate(zip(refs, scratch))]
    for copy in copies:
        copy.start()

    def wait(*which):
        for k in which:
            copies[k].wait()

    return wait


def store(pairs, sems):
    copies = [pltpu.make_async_copy(x, y, sems.at[k]) for k, (x, y) in enumerate(pairs)]
    for copy in copies:
        copy.start()
    return copies


def finish(copies):
    for copy in copies:
        copy.wait()


def frame_kernel(first, *refs):
    count = 7 if first else 14
    arrays, refs = refs[:count], refs[count:]
    if first:
        *stores, s1, s2, own = refs[:5]
        ext, canvas, raw, head, keep, send, outs, *inner, sems = refs[5:]
        up, mid, down, off, probe, amps, table = inner
    else:
        *stores, s1, s2, own, obj, probe_out = refs[:7]
        ext, canvas, raw, head, keep, send, outs, probe, *inner, sems = refs[7:]
        up, mid, down, off, ci, cm, co, di, do, probe_in, mine, other, amps, table = inner
    wait = fetch(arrays, inner, sems)
    canvas[...] = jnp.zeros(canvas.shape, f32)
    raw[...] = jnp.zeros(raw.shape, f32)
    wait(*range(4 if first else 9))
    o0 = off[0, 0, 0, 0]
    o1 = off[0, 0, 0, 1]
    row = lax.axis_index("row")
    col = lax.axis_index("col")
    core = lax.rem(col, 2)
    rest = lax.rem(o0, 8)
    base = pl.multiple_of(o0 - rest, 8)
    patch = []
    copies = []
    for c in range(2):
        whole = jnp.concatenate([up[c], mid[c], down[c]], axis=0)
        if not first:
            near, far = ci[c] + di[c], co[c] + do[c]
            grad = jnp.concatenate([choose(far, near), cm[c], choose(near, far)], axis=1)
            i = lax.broadcasted_iota(jnp.int32, (SPAN, SPAN), 0) + (row * TILE - H)
            j = lax.broadcasted_iota(jnp.int32, (SPAN, SPAN), 1) + (col * TILE - H)
            inside = (i >= 0) & (i < lax.axis_size("row") * TILE) & (j >= 0) & (
                j < lax.axis_size("col") * TILE)
            whole = jnp.where(inside, whole - object_step * grad, 0.0)
        ext[c, :SPAN, :] = whole
        ext[c, SPAN:, :] = jnp.zeros((8, SPAN), f32)
        rows = pltpu.roll(ext[c, pl.ds(base, F + 8), :], SPAN - o1, 1)[:, :F]
        patch.append(pltpu.roll(rows, F + 8 - rest, 0)[:F])
    pr, pi = patch
    if first:
        wait(4, 5, 6)
    else:
        wait(*range(9, 14))
        new_probe(core, probe_in, mine, other, probe)
        copies += store(
            ((ext.at[0, H:H + TILE], obj.at[0]), (ext.at[1, H:H + TILE], obj.at[1]),
             (probe, probe_out)), outs.at[10:13])
    right, left = blocks(table)
    wave = jnp.concatenate(
        [
            jnp.concatenate(
                [
                    probe[0, m] * pr - probe[1, m] * pi,
                    probe[0, m] * pi + probe[1, m] * pr,
                ],
                axis=1,
            )
            for m in range(M)
        ],
        axis=0,
    )
    x = product(split(wave), right)
    x = jnp.concatenate(
        [jnp.concatenate([x[m * F:(m + 1) * F, p * F:(p + 1) * F] for m in range(M)], axis=1)
         for p in range(2)], axis=0)
    x = product(left, split(x))
    square = x[:F] * x[:F] + x[F:] * x[F:]
    intensity = square[:, :F] + square[:, F:]
    factor = 1.0 - amps[0, 0, 0] * lax.rsqrt(intensity + 1.0)
    factor = jnp.concatenate([factor, factor], axis=1)
    x = jnp.concatenate([x[:F] * factor, x[F:] * factor], axis=0)
    x = product(right, split(x))
    x = jnp.concatenate(
        [jnp.concatenate([x[p * F:(p + 1) * F, m * F:(m + 1) * F] for p in range(2)], axis=1)
         for m in range(M)], axis=0)
    x = product(split(x), left)
    ore = jnp.zeros((F, F), f32)
    oim = jnp.zeros((F, F), f32)
    for m in range(M):
        br, bi = x[m * F:(m + 1) * F, :F], x[m * F:(m + 1) * F, F:]
        qr, qi = probe[0, m], probe[1, m]
        ore = ore + (qr * br + qi * bi)
        oim = oim + (qr * bi - qi * br)
        for p, term in enumerate((pr * br + pi * bi, pr * bi - pi * br)):
            s = slice((p * M + m) * F, (p * M + m + 1) * F)
            keep[s, :] = jnp.where(core == 0, term[:, :LANE], term[:, LANE:])
            send[s, :] = jnp.where(core == 0, term[:, LANE:], term[:, :LANE])
    copies += store(zip((keep, send), stores), outs.at[8:10])
    edge = (s1.shape[0] - 8) // 2
    at1 = pl.multiple_of(lax.rem(row + 1, 2) * (SPAN - edge), 8)
    at2 = pl.multiple_of(lax.rem(row, 2) * (SPAN - edge), 8)
    skip = (SPAN - own.shape[1]) // 2
    head[...] = jnp.full((8, F), o1.astype(f32))
    for c, value in enumerate((ore, oim)):
        value = jnp.concatenate([value, jnp.zeros((8, F), f32)], axis=0)
        value = pltpu.roll(value, rest, 0)
        raw[c, pl.ds(base, F + 8), :] = value
        s = slice(c * edge, (c + 1) * edge)
        copies += store(
            ((raw.at[c, pl.ds(at1, edge)], s1.at[s]), (raw.at[c, pl.ds(at2, edge)], s2.at[s])),
            outs.at[2 * c:2 * c + 2])
        canvas[c, pl.ds(base, F + 8), :] = shifted(value, o1)
        copies += store(((canvas.at[c, skip:SPAN - skip], own.at[c]),), outs.at[4 + c:5 + c])
    copies += store(((head, s1.at[2 * edge:]), (head, s2.at[2 * edge:])), outs.at[6:8])
    finish(copies)


def shifted(value, columns):
    value = jnp.concatenate([value, jnp.zeros((value.shape[0], SPAN - F), f32)], axis=1)
    return pltpu.roll(value, columns, 1)


def arrived(strip, c):
    edge = (strip.shape[0] - 8) // 2
    columns = jnp.max(strip[2 * edge:, :LANE]).astype(jnp.int32)
    return shifted(strip[c * edge:(c + 1) * edge, :], columns)


def above_below(r1, r2, c):
    x, y = arrived(r1, c), arrived(r2, c)
    even = lax.rem(lax.axis_index("row"), 2) == 0
    return jnp.where(even, y, x), jnp.where(even, x, y)


def new_probe(core, probe, mine, other, out):
    coeff = probe_step / (lax.axis_size("row") * lax.axis_size("col"))
    for q in range(4):
        s = slice(q * F, (q + 1) * F)
        x, y = mine[s, :], other[s, :]
        total = jnp.concatenate(
            [jnp.where(core == 0, x, y), jnp.where(core == 0, y, x)], axis=1)
        out[q // 2, q % 2] = probe[q // 2, q % 2] - coeff * total


def chunk_sum(parts, out):
    rows = out.shape[0]
    total = parts[:rows, :]
    for k in range(1, parts.shape[0] // rows):
        total = total + parts[k * rows:(k + 1) * rows, :]
    out[...] = total


def bands_kernel(parts, own, r1, r2, total, ci, cm, co, ti, tm, to, outs, *inner):
    *inner, sems = inner
    wait = fetch((own, r1, r2), inner, sems)
    own, r1, r2 = inner
    chunk_sum(parts, total)
    wait(*range(3))
    for c in range(2):
        above, below = above_below(r1, r2, c)
        rows = jnp.concatenate(
            [own[c, :B] + above, own[c, B:2 * B], own[c, 2 * B:] + below], axis=0)
        left, tm[c], right = rows[:, :B], rows[:, B:2 * B], rows[:, 2 * B:]
        ti[c] = choose(right, left)
        to[c] = choose(left, right)
    finish(store(zip((ti, to, tm), (ci, co, cm)), outs))


def last_bands_kernel(parts, own, r1, r2, total, grad_out, near, far, grad, outs, *inner):
    *inner, sems = inner
    wait = fetch((own, r1, r2), inner, sems)
    own, r1, r2 = inner
    chunk_sum(parts, total)
    low = lanes()
    wait(*range(3))
    for c in range(2):
        above, below = above_below(r1, r2, c)
        grad[c, :H] = own[c, :H] + above
        grad[c, H:TILE - H] = own[c, H:TILE - H]
        grad[c, TILE - H:] = own[c, TILE - H:] + below
    copies = store(((grad, grad_out),), outs)
    left = jnp.where(low, grad[0, :, :LANE], half_turn(grad[1, :, :LANE]))
    right = jnp.where(low, half_turn(grad[0, :, 2 * LANE:]), grad[1, :, 2 * LANE:])
    near[...] = choose(right, left)
    far[...] = choose(left, right)
    finish(copies)


def spread_kernel(a, b, c, d, out):
    total = (a[...] + b[...]) + (c[...] + d[...])
    rows = a.shape[0]
    for k in range(out.shape[0] // rows):
        out[k * rows:(k + 1) * rows, :] = total


def last_kernel(obj, grad, probe, near, far, mine, other, out, out_probe, *inner):
    *inner, sems = inner
    wait = fetch((obj, grad, probe), inner, sems)
    obj, grad, probe = inner
    low = lanes()
    west, east = choose(far[...], near[...]), choose(near[...], far[...])
    wait(*range(3))
    for c in range(2):
        w = half_turn(west) if c == 0 else west
        e = east if c == 0 else half_turn(east)
        x = obj[c, :, :LANE] - object_step * (grad[c, :, :LANE] + w)
        y = obj[c, :, LANE:2 * LANE] - object_step * grad[c, :, LANE:2 * LANE]
        z = obj[c, :, 2 * LANE:] - object_step * (grad[c, :, 2 * LANE:] + e)
        x, y, z = half_turn(x), half_turn(y), half_turn(z)
        out[c, :, :LANE] = jnp.where(low, x, y)
        out[c, :, LANE:] = jnp.where(low, y, z)
    new_probe(lax.rem(lax.axis_index("col"), 2), probe, mine, other, out_probe)


VM = pl.BlockSpec(memory_space=pltpu.VMEM)
HBM = pl.BlockSpec(memory_space=pltpu.HBM)


def call(kernel, outs, name, limit=SMALL_LIMIT, specs=(), places=(), scratch=()):
    def run(*args):
        held = list(specs) or [VM] * len(args)
        inner = [
            (pltpu.VMEM if x.dtype != jnp.int32 else pltpu.SMEM)(x.shape, x.dtype)
            for x, s in zip(args, held) if s is HBM
        ]
        if inner:
            inner.append(pltpu.SemaphoreType.DMA((len(inner),)))
        return pl.pallas_call(
            kernel,
            out_shape=[jax.ShapeDtypeStruct(s, f32) for s in outs],
            in_specs=held,
            out_specs=list(places) or [VM] * len(outs),
            scratch_shapes=list(scratch) + inner,
            compiler_params=pltpu.CompilerParams(vmem_limit_bytes=limit),
            name=name,
        )(*args)

    return run


def shift(x, axis, step):
    count = lax.axis_size(axis)
    pairs = [(i, i + step) for i in range(count) if 0 <= i + step < count]
    return lax.ppermute(x, axis, pairs)


def exchange(x, mask):
    return lax.ppermute(x, RC, [(i, i ^ mask) for i in range(256)])


def add_kernel(keep, arrived_half, out, total, outs, *inner):
    *inner, sems = inner
    fetch((keep, arrived_half), inner, sems)(0, 1)
    total[...] = inner[0][...] + inner[1][...]
    finish(store(((total, out),), outs))


def columns(near, far):
    count = lax.axis_size("col")
    pairs = [(i, i + 1) for i in range(1, count - 1, 2)]
    pairs += [(j, i) for i, j in pairs]
    return exchange(near, BIT_CORE), lax.ppermute(far, "col", pairs)


def groups(mask):
    members = [i for i in range(256) if i & ~mask == 0]
    return [[base | i for i in members] for base in range(256) if base & mask == 0]


WIDE = BIT_Y | BIT_ZLO | BIT_X
COUNT = 32
CHUNK = 1024 // COUNT


def scatter(keep, send, s1, s2):
    count = lax.axis_size("row")
    pairs = [(i, i + 1) for i in range(1, count - 1, 2)]
    pairs += [(j, i) for i, j in pairs]
    recv, r1 = lax.optimization_barrier((exchange(send, BIT_CORE), exchange(s1, BIT_ZLO)))
    (x,) = call(
        add_kernel,
        [(1024, LANE)],
        "add",
        specs=[HBM] * 2,
        places=[HBM],
        scratch=[pltpu.VMEM((1024, LANE), f32), pltpu.SemaphoreType.DMA((1,))],
    )(keep, recv)
    x = lax.all_to_all(x, RC, 0, 0, axis_index_groups=groups(WIDE), tiled=True)
    return x, r1, lax.ppermute(s2, "row", pairs)


def gather(x, *early):
    parts = (x, exchange(x, 2), exchange(x, 4), exchange(x, 6))
    parts, early = lax.optimization_barrier((parts, early))
    (x,) = call(spread_kernel, [(1024, LANE)], "spread")(*parts)
    x = lax.all_to_all(x, RC, 0, 0, axis_index_groups=groups(WIDE), tiled=True)
    return x, exchange(x, BIT_CORE), *early


def local(object_field, probe, amplitudes, offsets):
    table = tables()
    sides = call(sides_kernel, [(TILE, LANE)] * 2, "sides")(object_field)
    mid, top, bottom = call(
        rows_kernel, [(2, TILE, SPAN)] + [(2, H, SPAN)] * 2, "rows"
    )(object_field, *columns(*sides))
    up = shift(bottom, "row", 1)
    down = shift(top, "row", -1)

    halves = [(1024, LANE)] * 2
    held = [pltpu.VMEM((2, SPAN + 8, SPAN), f32)] * 2 + [pltpu.VMEM((2, SPAN + 8, F), f32)]
    held += [pltpu.VMEM((8, F), f32)] + [pltpu.VMEM((1024, LANE), f32)] * 2
    keep, send, s1, s2, own = call(
        functools.partial(frame_kernel, True),
        halves + [(2 * B + 8, F)] * 2 + [(2, SPAN, SPAN)],
        "frame1",
        VMEM_LIMIT,
        [HBM] * 7,
        [HBM] * 5,
        held + [pltpu.SemaphoreType.DMA((10,))],
    )(up, mid, down, offsets, probe, amplitudes, table)
    parts, r1, r2 = scatter(keep, send, s1, s2)
    total, ci, cm, co = call(
        bands_kernel,
        [(CHUNK, LANE)] + [(2, SPAN, B)] * 3,
        "bands",
        specs=[VM] + [HBM] * 3,
        places=[VM] + [HBM] * 3,
        scratch=[pltpu.VMEM((2, SPAN, B), f32)] * 3 + [pltpu.SemaphoreType.DMA((3,))],
    )(parts, own, r1, r2)
    mine, other, di, do = gather(total, *columns(ci, co))

    keep, send, s1, s2, own, obj, probe = call(
        functools.partial(frame_kernel, False),
        halves + [(2 * H + 8, F)] * 2 + [(2, TILE, SPAN)] * 2 + [(2, M, F, F)],
        "frame2",
        VMEM_LIMIT,
        [HBM] * 14,
        [HBM] * 7,
        held + [pltpu.SemaphoreType.DMA((13,)), pltpu.VMEM((2, M, F, F), f32)],
    )(up, mid, down, offsets, ci, cm, co, di, do, probe, mine, other, amplitudes, table)
    parts, r1, r2 = scatter(keep, send, s1, s2)
    total, grad, near, far = call(
        last_bands_kernel,
        [(CHUNK, LANE), (2, TILE, SPAN)] + [(TILE, LANE)] * 2,
        "last_bands",
        specs=[VM] + [HBM] * 3,
        places=[VM, HBM, VM, VM],
        scratch=[pltpu.VMEM((2, TILE, SPAN), f32), pltpu.SemaphoreType.DMA((1,))],
    )(parts, own, r1, r2)
    mine, other, near, far = gather(total, *columns(near, far))
    return tuple(
        call(
            last_kernel,
            [(2, TILE, TILE), (2, M, F, F)],
            "last",
            specs=[HBM] * 3 + [VM] * 4,
        )(obj, grad, probe, near, far, mine, other)
    )


def solution(mesh):
    return jax.shard_map(
        local,
        mesh=mesh,
        in_specs=(
            P(None, "row", "col"),
            P(),
            P("row", "col", None, None, None),
            P("row", "col", None, None),
        ),
        out_specs=(P(None, "row", "col"), P()),
        check_vma=False,
    )
```

```python
import functools
import math

import jax
import jax.numpy as jnp
import ml_dtypes
import numpy as np
from jax import lax
from jax.experimental import pallas as pl
from jax.experimental.pallas import tpu as pltpu
from jax.sharding import PartitionSpec as P

H = 64
F = 256
M = 2
TILE = 256
SPAN = TILE + 2 * H
B = 2 * H
object_step = 0.25
probe_step = 4.0
RC = ("row", "col")
BIT_Y, BIT_ZLO, BIT_X, BIT_ZHI, BIT_CORE = 192, 32, 24, 6, 1

COUNT, DEPTH = 16, 8
CHUNK = 1024 // COUNT

f32 = jnp.float32
bf16 = jnp.bfloat16
VMEM_LIMIT = 56 * 1024 * 1024
SMALL_LIMIT = 24 * 1024 * 1024


def tables():
    counter = np.arange(F)
    angle = -2.0 * math.pi / F * (counter[:, None] * counter[None, :] % F)
    out = []
    for table in (np.cos(angle) / math.sqrt(F), np.sin(angle) / math.sqrt(F)):
        high = table.astype(np.float32).astype(ml_dtypes.bfloat16)
        low = (table - high.astype(np.float64)).astype(np.float32).astype(ml_dtypes.bfloat16)
        out += [high, low]
    return np.concatenate(out, axis=0)


def blocks(table):
    rh, rl, ih, il = (table[k * F:(k + 1) * F, :] for k in range(4))

    def block(re, im, under):
        return jnp.concatenate(
            [jnp.concatenate([re, im], axis=1), jnp.concatenate([under, re], axis=1)], axis=0)

    return (block(rh, ih, -ih), block(rl, il, -il)), (block(rh, -ih, ih), block(rl, -il, il))


def split(x):
    high = x.astype(bf16)
    return high, (x - high.astype(f32)).astype(bf16)


def dot(a, b):
    return jnp.dot(a, b, preferred_element_type=f32)


def product(left, right):
    return dot(left[0], right[0]) + (dot(left[0], right[1]) + dot(left[1], right[0]))


LANE = 128


def lanes():
    return lax.broadcasted_iota(jnp.int32, (TILE, LANE), 1) < H


def half_turn(x):
    return pltpu.roll(x, H, 1)


def core_index():
    return lax.rem(lax.axis_index("col"), 2)


def choose(x, y):
    return jnp.where(core_index() == 0, x, y)


def sides_kernel(obj, inner, outer):
    low = lanes()
    left = jnp.where(low, obj[0, :, :LANE], half_turn(obj[1, :, :LANE]))
    right = jnp.where(low, half_turn(obj[0, :, LANE:]), obj[1, :, LANE:])
    inner[...] = choose(right, left)
    outer[...] = choose(left, right)


def rows_kernel(obj, inner, outer, mid, top, bottom):
    low = lanes()
    west, east = choose(outer[...], inner[...]), choose(inner[...], outer[...])
    for c in range(2):
        x, y = half_turn(obj[c, :, :LANE]), half_turn(obj[c, :, LANE:])
        w = west if c == 0 else half_turn(west)
        e = half_turn(east) if c == 0 else east
        for k, part in enumerate((jnp.where(low, w, x), jnp.where(low, x, y), jnp.where(low, y, e))):
            s = slice(k * LANE, (k + 1) * LANE)
            mid[c, :, s] = part
            top[c, :, s] = part[:H]
            bottom[c, :, s] = part[TILE - H:]


def fetch(refs, scratch, sems):
    copies = [pltpu.make_async_copy(r, t, sems.at[k]) for k, (r, t) in enumerate(zip(refs, scratch))]
    for copy in copies:
        copy.start()

    def wait(*which):
        for k in which:
            copies[k].wait()

    return wait


def store(pairs, sems):
    copies = [pltpu.make_async_copy(x, y, sems.at[k]) for k, (x, y) in enumerate(pairs)]
    for copy in copies:
        copy.start()
    return copies


def finish(copies):
    for copy in copies:
        copy.wait()


def frame_kernel(first, *refs):
    count = 7 if first else 14
    arrays, refs = refs[:count], refs[count:]
    if first:
        *stores, su, sd, own = refs[:5]
        ext, canvas, raw, head, keep, send, outs, *inner, sems = refs[5:]
        up, mid, down, off, probe, amps, table = inner
    else:
        *stores, su, sd, own, obj, probe_out = refs[:7]
        ext, canvas, raw, head, keep, send, outs, probe, *inner, sems = refs[7:]
        up, mid, down, off, ci, cm, co, di, do, probe_in, mine, other, amps, table = inner
    wait = fetch(arrays, inner, sems)
    wait(*range(4 if first else 9))
    o0 = off[0, 0, 0, 0]
    o1 = off[0, 0, 0, 1]
    row = lax.axis_index("row")
    col = lax.axis_index("col")
    core = lax.rem(col, 2)
    rest = lax.rem(o0, 8)
    base = pl.multiple_of(o0 - rest, 8)
    patch = []
    copies = []
    for c in range(2):
        whole = jnp.concatenate([up[c], mid[c], down[c]], axis=0)
        if not first:
            near, far = ci[c] + di[c], co[c] + do[c]
            grad = jnp.concatenate([choose(far, near), cm[c], choose(near, far)], axis=1)
            i = lax.broadcasted_iota(jnp.int32, (SPAN, SPAN), 0) + (row * TILE - H)
            j = lax.broadcasted_iota(jnp.int32, (SPAN, SPAN), 1) + (col * TILE - H)
            inside = (i >= 0) & (i < lax.axis_size("row") * TILE) & (j >= 0) & (
                j < lax.axis_size("col") * TILE)
            whole = jnp.where(inside, whole - object_step * grad, 0.0)
        ext[c, :SPAN, :] = whole
        ext[c, SPAN:, :] = jnp.zeros((8, SPAN), f32)
        rows = pltpu.roll(ext[c, pl.ds(base, F + 8), :], SPAN - o1, 1)[:, :F]
        patch.append(pltpu.roll(rows, F + 8 - rest, 0)[:F])
    pr, pi = patch
    if first:
        wait(4, 5, 6)
    else:
        wait(*range(9, 14))
        new_probe(core, probe_in, mine, other, probe)
        copies += store(
            ((ext.at[0, H:H + TILE], obj.at[0]), (ext.at[1, H:H + TILE], obj.at[1]),
             (probe, probe_out)), outs.at[10:13])
    right, left = blocks(table)
    wave = jnp.concatenate(
        [
            jnp.concatenate(
                [
                    probe[0, m] * pr - probe[1, m] * pi,
                    probe[0, m] * pi + probe[1, m] * pr,
                ],
                axis=1,
            )
            for m in range(M)
        ],
        axis=0,
    )
    x = product(split(wave), right)
    x = jnp.concatenate(
        [jnp.concatenate([x[m * F:(m + 1) * F, p * F:(p + 1) * F] for m in range(M)], axis=1)
         for p in range(2)], axis=0)
    x = product(left, split(x))
    square = x[:F] * x[:F] + x[F:] * x[F:]
    intensity = square[:, :F] + square[:, F:]
    factor = 1.0 - amps[0, 0, 0] * lax.rsqrt(intensity + 1.0)
    factor = jnp.concatenate([factor, factor], axis=1)
    x = jnp.concatenate([x[:F] * factor, x[F:] * factor], axis=0)
    x = product(right, split(x))
    x = jnp.concatenate(
        [jnp.concatenate([x[p * F:(p + 1) * F, m * F:(m + 1) * F] for p in range(2)], axis=1)
         for m in range(M)], axis=0)
    x = product(split(x), left)
    ore = jnp.zeros((F, F), f32)
    oim = jnp.zeros((F, F), f32)
    for m in range(M):
        br, bi = x[m * F:(m + 1) * F, :F], x[m * F:(m + 1) * F, F:]
        qr, qi = probe[0, m], probe[1, m]
        ore = ore + (qr * br + qi * bi)
        oim = oim + (qr * bi - qi * br)
        for p, term in enumerate((pr * br + pi * bi, pr * bi - pi * br)):
            s = slice((p * M + m) * F, (p * M + m + 1) * F)
            keep[s, :] = jnp.where(core == 0, term[:, :LANE], term[:, LANE:])
            send[s, :] = jnp.where(core == 0, term[:, LANE:], term[:, :LANE])
    copies += store(zip((keep, send), stores), outs.at[8:10])
    edge = (su.shape[0] - 8) // 2
    skip = (SPAN - own.shape[1]) // 2
    head[...] = jnp.full((8, F), o1.astype(f32))
    for c, value in enumerate((ore, oim)):
        canvas[c] = jnp.zeros((SPAN + 8, SPAN), f32)
        raw[c] = jnp.zeros((SPAN + 8, F), f32)
        value = jnp.concatenate([value, jnp.zeros((8, F), f32)], axis=0)
        value = pltpu.roll(value, rest, 0)
        raw[c, pl.ds(base, F + 8), :] = value
        s = slice(c * edge, (c + 1) * edge)
        copies += store(
            ((raw.at[c, :edge], su.at[s]), (raw.at[c, SPAN - edge:SPAN], sd.at[s])),
            outs.at[2 * c:2 * c + 2])
        canvas[c, pl.ds(base, F + 8), :] = shifted(value, o1)
        copies += store(((canvas.at[c, skip:SPAN - skip], own.at[c]),), outs.at[4 + c:5 + c])
    copies += store(((head, su.at[2 * edge:]), (head, sd.at[2 * edge:])), outs.at[6:8])
    finish(copies)


def shifted(value, columns):
    value = jnp.concatenate([value, jnp.zeros((value.shape[0], SPAN - F), f32)], axis=1)
    return pltpu.roll(value, columns, 1)


def arrived(strip, c):
    edge = (strip.shape[0] - 8) // 2
    columns = jnp.max(strip[2 * edge:, :LANE]).astype(jnp.int32)
    return shifted(strip[c * edge:(c + 1) * edge, :], columns)


def new_probe(core, probe, mine, other, out):
    coeff = probe_step / (lax.axis_size("row") * lax.axis_size("col"))
    for q in range(4):
        s = slice(q * F, (q + 1) * F)
        x, y = mine[s, :], other[s, :]
        total = jnp.concatenate(
            [jnp.where(core == 0, x, y), jnp.where(core == 0, y, x)], axis=1)
        out[q // 2, q % 2] = probe[q // 2, q % 2] - coeff * total


def chunk_sum(parts, count, out):
    rows = parts.shape[0] // count
    total = parts[:rows, :]
    for k in range(1, count):
        total = total + parts[k * rows:(k + 1) * rows, :]
    for k in range(out.shape[0] // rows):
        out[k * rows:(k + 1) * rows, :] = total


def bands_kernel(parts, own, ru, rd, total, ci, cm, co, ti, tm, to, outs, *inner):
    *inner, sems = inner
    wait = fetch((own, ru, rd), inner, sems)
    own, ru, rd = inner
    chunk_sum(parts, COUNT, total)
    wait(*range(3))
    for c in range(2):
        rows = jnp.concatenate(
            [own[c, :B] + arrived(ru, c), own[c, B:2 * B], own[c, 2 * B:] + arrived(rd, c)], axis=0)
        left, tm[c], right = rows[:, :B], rows[:, B:2 * B], rows[:, 2 * B:]
        ti[c] = choose(right, left)
        to[c] = choose(left, right)
    finish(store(zip((ti, to, tm), (ci, co, cm)), outs))


def last_bands_kernel(parts, own, ru, rd, total, grad_out, near, far, grad, outs, *inner):
    *inner, sems = inner
    wait = fetch((own, ru, rd), inner, sems)
    own, ru, rd = inner
    chunk_sum(parts, COUNT, total)
    low = lanes()
    wait(*range(3))
    for c in range(2):
        grad[c, :H] = own[c, :H] + arrived(ru, c)
        grad[c, H:TILE - H] = own[c, H:TILE - H]
        grad[c, TILE - H:] = own[c, TILE - H:] + arrived(rd, c)
    copies = store(((grad, grad_out),), outs)
    left = jnp.where(low, grad[0, :, :LANE], half_turn(grad[1, :, :LANE]))
    right = jnp.where(low, half_turn(grad[0, :, 2 * LANE:]), grad[1, :, 2 * LANE:])
    near[...] = choose(right, left)
    far[...] = choose(left, right)
    finish(copies)


def spread_kernel(parts, out):
    chunk_sum(parts, DEPTH, out)


def last_kernel(obj, grad, probe, near, far, mine, other, out, out_probe, *inner):
    *inner, sems = inner
    wait = fetch((obj, grad, probe), inner, sems)
    obj, grad, probe = inner
    low = lanes()
    west, east = choose(far[...], near[...]), choose(near[...], far[...])
    wait(*range(3))
    for c in range(2):
        w = half_turn(west) if c == 0 else west
        e = east if c == 0 else half_turn(east)
        x = obj[c, :, :LANE] - object_step * (grad[c, :, :LANE] + w)
        y = obj[c, :, LANE:2 * LANE] - object_step * grad[c, :, LANE:2 * LANE]
        z = obj[c, :, 2 * LANE:] - object_step * (grad[c, :, 2 * LANE:] + e)
        x, y, z = half_turn(x), half_turn(y), half_turn(z)
        out[c, :, :LANE] = jnp.where(low, x, y)
        out[c, :, LANE:] = jnp.where(low, y, z)
    new_probe(lax.rem(lax.axis_index("col"), 2), probe, mine, other, out_probe)


VM = pl.BlockSpec(memory_space=pltpu.VMEM)
HBM = pl.BlockSpec(memory_space=pltpu.HBM)


def call(kernel, outs, name, limit=SMALL_LIMIT, specs=(), places=(), scratch=()):
    def run(*args):
        held = list(specs) or [VM] * len(args)
        inner = [
            (pltpu.VMEM if x.dtype != jnp.int32 else pltpu.SMEM)(x.shape, x.dtype)
            for x, s in zip(args, held) if s is HBM
        ]
        if inner:
            inner.append(pltpu.SemaphoreType.DMA((len(inner),)))
        return pl.pallas_call(
            kernel,
            out_shape=[jax.ShapeDtypeStruct(s, f32) for s in outs],
            in_specs=held,
            out_specs=list(places) or [VM] * len(outs),
            scratch_shapes=list(scratch) + inner,
            compiler_params=pltpu.CompilerParams(vmem_limit_bytes=limit),
            name=name,
        )(*args)

    return run


def shift(x, axis, step):
    count = lax.axis_size(axis)
    pairs = [(i, i + step) for i in range(count) if 0 <= i + step < count]
    return lax.ppermute(x, axis, pairs)


def exchange(x, mask):
    return lax.ppermute(x, RC, [(i, i ^ mask) for i in range(256)])


def columns(near, far):
    count = lax.axis_size("col")
    pairs = [(i, i + 1) for i in range(1, count - 1, 2)]
    pairs += [(j, i) for i, j in pairs]
    return exchange(near, BIT_CORE), lax.ppermute(far, "col", pairs)


def groups(mask):
    members = [i for i in range(256) if i & ~mask == 0]
    return [[base | i for i in members] for base in range(256) if base & mask == 0]


def all_to_all(x, mask):
    return lax.all_to_all(x, RC, 0, 0, axis_index_groups=groups(mask), tiled=True)


def scatter(keep, send):
    return all_to_all(keep + exchange(send, BIT_CORE), BIT_Y | BIT_X)


def gather(x, *early):
    x = all_to_all(x, BIT_ZLO | BIT_ZHI)
    x, early = lax.optimization_barrier((x, early))
    (x,) = call(spread_kernel, [(1024, LANE)], "spread")(x)
    x = all_to_all(x, BIT_Y | BIT_X)
    return x, exchange(x, BIT_CORE), *early


def local(object_field, probe, amplitudes, offsets):
    table = tables()
    sides = call(sides_kernel, [(TILE, LANE)] * 2, "sides")(object_field)
    mid, top, bottom = call(
        rows_kernel, [(2, TILE, SPAN)] + [(2, H, SPAN)] * 2, "rows"
    )(object_field, *columns(*sides))
    up = shift(bottom, "row", 1)
    down = shift(top, "row", -1)

    halves = [(1024, LANE)] * 2
    held = [pltpu.VMEM((2, SPAN + 8, SPAN), f32)] * 2 + [pltpu.VMEM((2, SPAN + 8, F), f32)]
    held += [pltpu.VMEM((8, F), f32)] + [pltpu.VMEM((1024, LANE), f32)] * 2
    keep, send, su, sd, own = call(
        functools.partial(frame_kernel, True),
        halves + [(2 * B + 8, F)] * 2 + [(2, SPAN, SPAN)],
        "frame1",
        VMEM_LIMIT,
        [HBM] * 7,
        [HBM] * 5,
        held + [pltpu.SemaphoreType.DMA((10,))],
    )(up, mid, down, offsets, probe, amplitudes, table)
    ru = shift(sd, "row", 1)
    rd = shift(su, "row", -1)
    total, ci, cm, co = call(
        bands_kernel,
        [(DEPTH * CHUNK, LANE)] + [(2, SPAN, B)] * 3,
        "bands",
        specs=[VM] + [HBM] * 3,
        places=[VM] + [HBM] * 3,
        scratch=[pltpu.VMEM((2, SPAN, B), f32)] * 3 + [pltpu.SemaphoreType.DMA((3,))],
    )(scatter(keep, send), own, ru, rd)
    mine, other, di, do = gather(total, *columns(ci, co))

    keep, send, su, sd, own, obj, probe = call(
        functools.partial(frame_kernel, False),
        halves + [(2 * H + 8, F)] * 2 + [(2, TILE, SPAN)] * 2 + [(2, M, F, F)],
        "frame2",
        VMEM_LIMIT,
        [HBM] * 14,
        [HBM] * 7,
        held + [pltpu.SemaphoreType.DMA((13,)), pltpu.VMEM((2, M, F, F), f32)],
    )(up, mid, down, offsets, ci, cm, co, di, do, probe, mine, other, amplitudes, table)
    ru = shift(sd, "row", 1)
    rd = shift(su, "row", -1)
    total, grad, near, far = call(
        last_bands_kernel,
        [(DEPTH * CHUNK, LANE), (2, TILE, SPAN)] + [(TILE, LANE)] * 2,
        "last_bands",
        specs=[VM] + [HBM] * 3,
        places=[VM, HBM, VM, VM],
        scratch=[pltpu.VMEM((2, TILE, SPAN), f32), pltpu.SemaphoreType.DMA((1,))],
    )(scatter(keep, send), own, ru, rd)
    mine, other, near, far = gather(total, *columns(near, far))
    return tuple(
        call(
            last_kernel,
            [(2, TILE, TILE), (2, M, F, F)],
            "last",
            specs=[HBM] * 3 + [VM] * 4,
        )(obj, grad, probe, near, far, mine, other)
    )


def solution(mesh):
    return jax.shard_map(
        local,
        mesh=mesh,
        in_specs=(
            P(None, "row", "col"),
            P(),
            P("row", "col", None, None, None),
            P("row", "col", None, None),
        ),
        out_specs=(P(None, "row", "col"), P()),
        check_vma=False,
    )
```

```python
import functools
import math

import jax
import jax.numpy as jnp
import ml_dtypes
import numpy as np
from jax import lax
from jax.experimental import pallas as pl
from jax.experimental.pallas import tpu as pltpu
from jax.sharding import PartitionSpec as P

H = 64
F = 256
M = 2
TILE = 256
SPAN = TILE + 2 * H
B = 2 * H
object_step = 0.25
probe_step = 4.0
RC = ("row", "col")
BIT_Y, BIT_ZLO, BIT_X, BIT_ZHI, BIT_CORE = 192, 32, 24, 6, 1

f32 = jnp.float32
bf16 = jnp.bfloat16
VMEM_LIMIT = 56 * 1024 * 1024
SMALL_LIMIT = 24 * 1024 * 1024


def tables():
    counter = np.arange(F)
    angle = -2.0 * math.pi / F * (counter[:, None] * counter[None, :] % F)
    out = []
    for table in (np.cos(angle) / math.sqrt(F), np.sin(angle) / math.sqrt(F)):
        high = table.astype(np.float32).astype(ml_dtypes.bfloat16)
        low = (table - high.astype(np.float64)).astype(np.float32).astype(ml_dtypes.bfloat16)
        out += [high, low]
    return np.concatenate(out, axis=0)


def blocks(table):
    rh, rl, ih, il = (table[k * F:(k + 1) * F, :] for k in range(4))

    def block(re, im, under):
        return jnp.concatenate(
            [jnp.concatenate([re, im], axis=1), jnp.concatenate([under, re], axis=1)], axis=0)

    return (block(rh, ih, -ih), block(rl, il, -il)), (block(rh, -ih, ih), block(rl, -il, il))


def split(x):
    high = x.astype(bf16)
    return high, (x - high.astype(f32)).astype(bf16)


def dot(a, b):
    return jnp.dot(a, b, preferred_element_type=f32)


def product(left, right):
    return dot(left[0], right[0]) + (dot(left[0], right[1]) + dot(left[1], right[0]))


LANE = 128


def lanes():
    return lax.broadcasted_iota(jnp.int32, (TILE, LANE), 1) < H


def half_turn(x):
    return pltpu.roll(x, H, 1)


def core_index():
    return lax.rem(lax.axis_index("col"), 2)


def choose(x, y):
    return jnp.where(core_index() == 0, x, y)


def sides_kernel(obj, inner, outer):
    low = lanes()
    left = jnp.where(low, obj[0, :, :LANE], half_turn(obj[1, :, :LANE]))
    right = jnp.where(low, half_turn(obj[0, :, LANE:]), obj[1, :, LANE:])
    inner[...] = choose(right, left)
    outer[...] = choose(left, right)


def rows_kernel(obj, inner, outer, mid, top, bottom):
    low = lanes()
    west, east = choose(outer[...], inner[...]), choose(inner[...], outer[...])
    for c in range(2):
        x, y = half_turn(obj[c, :, :LANE]), half_turn(obj[c, :, LANE:])
        w = west if c == 0 else half_turn(west)
        e = half_turn(east) if c == 0 else east
        for k, part in enumerate((jnp.where(low, w, x), jnp.where(low, x, y), jnp.where(low, y, e))):
            s = slice(k * LANE, (k + 1) * LANE)
            mid[c, :, s] = part
            top[c, :, s] = part[:H]
            bottom[c, :, s] = part[TILE - H:]


def fetch(refs, scratch, sems):
    copies = [pltpu.make_async_copy(r, t, sems.at[k]) for k, (r, t) in enumerate(zip(refs, scratch))]
    for copy in copies:
        copy.start()

    def wait(*which):
        for k in which:
            copies[k].wait()

    return wait


def store(pairs, sems):
    copies = [pltpu.make_async_copy(x, y, sems.at[k]) for k, (x, y) in enumerate(pairs)]
    for copy in copies:
        copy.start()
    return copies


def finish(copies):
    for copy in copies:
        copy.wait()


def frame_kernel(first, *refs):
    count = 7 if first else 14
    arrays, refs = refs[:count], refs[count:]
    if first:
        *stores, su, sd, own = refs[:5]
        ext, canvas, raw, head, keep, send, outs, *inner, sems = refs[5:]
        up, mid, down, off, probe, amps, table = inner
    else:
        *stores, su, sd, own, obj, probe_out = refs[:7]
        ext, canvas, raw, head, keep, send, outs, probe, *inner, sems = refs[7:]
        up, mid, down, off, ci, cm, co, di, do, probe_in, mine, other, amps, table = inner
    wait = fetch(arrays, inner, sems)
    wait(*range(4 if first else 9))
    o0 = off[0, 0, 0, 0]
    o1 = off[0, 0, 0, 1]
    row = lax.axis_index("row")
    col = lax.axis_index("col")
    core = lax.rem(col, 2)
    rest = lax.rem(o0, 8)
    base = pl.multiple_of(o0 - rest, 8)
    patch = []
    copies = []
    for c in range(2):
        whole = jnp.concatenate([up[c], mid[c], down[c]], axis=0)
        if not first:
            near, far = ci[c] + di[c], co[c] + do[c]
            grad = jnp.concatenate([choose(far, near), cm[c], choose(near, far)], axis=1)
            i = lax.broadcasted_iota(jnp.int32, (SPAN, SPAN), 0) + (row * TILE - H)
            j = lax.broadcasted_iota(jnp.int32, (SPAN, SPAN), 1) + (col * TILE - H)
            inside = (i >= 0) & (i < lax.axis_size("row") * TILE) & (j >= 0) & (
                j < lax.axis_size("col") * TILE)
            whole = jnp.where(inside, whole - object_step * grad, 0.0)
        ext[c, :SPAN, :] = whole
        ext[c, SPAN:, :] = jnp.zeros((8, SPAN), f32)
        rows = pltpu.roll(ext[c, pl.ds(base, F + 8), :], SPAN - o1, 1)[:, :F]
        patch.append(pltpu.roll(rows, F + 8 - rest, 0)[:F])
    pr, pi = patch
    if first:
        wait(4, 5, 6)
    else:
        wait(*range(9, 14))
        new_probe(core, probe_in, mine, other, probe)
        copies += store(
            ((ext.at[0, H:H + TILE], obj.at[0]), (ext.at[1, H:H + TILE], obj.at[1]),
             (probe, probe_out)), outs.at[10:13])
    right, left = blocks(table)
    wave = jnp.concatenate(
        [
            jnp.concatenate(
                [
                    probe[0, m] * pr - probe[1, m] * pi,
                    probe[0, m] * pi + probe[1, m] * pr,
                ],
                axis=1,
            )
            for m in range(M)
        ],
        axis=0,
    )
    x = product(split(wave), right)
    x = jnp.concatenate(
        [jnp.concatenate([x[m * F:(m + 1) * F, p * F:(p + 1) * F] for m in range(M)], axis=1)
         for p in range(2)], axis=0)
    x = product(left, split(x))
    square = x[:F] * x[:F] + x[F:] * x[F:]
    intensity = square[:, :F] + square[:, F:]
    factor = 1.0 - amps[0, 0, 0] * lax.rsqrt(intensity + 1.0)
    factor = jnp.concatenate([factor, factor], axis=1)
    x = jnp.concatenate([x[:F] * factor, x[F:] * factor], axis=0)
    x = product(right, split(x))
    x = jnp.concatenate(
        [jnp.concatenate([x[p * F:(p + 1) * F, m * F:(m + 1) * F] for p in range(2)], axis=1)
         for m in range(M)], axis=0)
    x = product(split(x), left)
    ore = jnp.zeros((F, F), f32)
    oim = jnp.zeros((F, F), f32)
    for m in range(M):
        br, bi = x[m * F:(m + 1) * F, :F], x[m * F:(m + 1) * F, F:]
        qr, qi = probe[0, m], probe[1, m]
        ore = ore + (qr * br + qi * bi)
        oim = oim + (qr * bi - qi * br)
        for p, term in enumerate((pr * br + pi * bi, pr * bi - pi * br)):
            s = slice((p * M + m) * F, (p * M + m + 1) * F)
            keep[s, :] = jnp.where(core == 0, term[:, :LANE], term[:, LANE:])
            send[s, :] = jnp.where(core == 0, term[:, LANE:], term[:, :LANE])
    copies += store(zip((keep, send), stores), outs.at[8:10])
    edge = (su.shape[0] - 8) // 2
    skip = (SPAN - own.shape[1]) // 2
    head[...] = jnp.full((8, F), o1.astype(f32))
    for c, value in enumerate((ore, oim)):
        canvas[c] = jnp.zeros((SPAN + 8, SPAN), f32)
        raw[c] = jnp.zeros((SPAN + 8, F), f32)
        value = jnp.concatenate([value, jnp.zeros((8, F), f32)], axis=0)
        value = pltpu.roll(value, rest, 0)
        raw[c, pl.ds(base, F + 8), :] = value
        s = slice(c * edge, (c + 1) * edge)
        copies += store(
            ((raw.at[c, :edge], su.at[s]), (raw.at[c, SPAN - edge:SPAN], sd.at[s])),
            outs.at[2 * c:2 * c + 2])
        canvas[c, pl.ds(base, F + 8), :] = shifted(value, o1)
        copies += store(((canvas.at[c, skip:SPAN - skip], own.at[c]),), outs.at[4 + c:5 + c])
    copies += store(((head, su.at[2 * edge:]), (head, sd.at[2 * edge:])), outs.at[6:8])
    finish(copies)


def shifted(value, columns):
    value = jnp.concatenate([value, jnp.zeros((value.shape[0], SPAN - F), f32)], axis=1)
    return pltpu.roll(value, columns, 1)


def arrived(strip, c):
    edge = (strip.shape[0] - 8) // 2
    columns = jnp.max(strip[2 * edge:, :LANE]).astype(jnp.int32)
    return shifted(strip[c * edge:(c + 1) * edge, :], columns)


def new_probe(core, probe, mine, other, out):
    coeff = probe_step / (lax.axis_size("row") * lax.axis_size("col"))
    for q in range(4):
        s = slice(q * F, (q + 1) * F)
        x, y = mine[s, :], other[s, :]
        total = jnp.concatenate(
            [jnp.where(core == 0, x, y), jnp.where(core == 0, y, x)], axis=1)
        out[q // 2, q % 2] = probe[q // 2, q % 2] - coeff * total


def spread(parts, out):
    a, b, c, d = parts
    total = (a[...] + b[...]) + (c[...] + d[...])
    rows = a.shape[0]
    for k in range(out.shape[0] // rows):
        out[k * rows:(k + 1) * rows, :] = total


def bands_kernel(p0, p1, p2, p3, own, ru, rd, total, ci, cm, co, ti, tm, to, outs, *inner):
    *inner, sems = inner
    wait = fetch((own, ru, rd), inner, sems)
    own, ru, rd = inner
    spread((p0, p1, p2, p3), total)
    wait(*range(3))
    for c in range(2):
        rows = jnp.concatenate(
            [own[c, :B] + arrived(ru, c), own[c, B:2 * B], own[c, 2 * B:] + arrived(rd, c)], axis=0)
        left, tm[c], right = rows[:, :B], rows[:, B:2 * B], rows[:, 2 * B:]
        ti[c] = choose(right, left)
        to[c] = choose(left, right)
    finish(store(zip((ti, to, tm), (ci, co, cm)), outs))


def last_bands_kernel(p0, p1, p2, p3, own, ru, rd, total, grad_out, near, far, grad, outs, *inner):
    *inner, sems = inner
    wait = fetch((own, ru, rd), inner, sems)
    own, ru, rd = inner
    spread((p0, p1, p2, p3), total)
    low = lanes()
    wait(*range(3))
    for c in range(2):
        grad[c, :H] = own[c, :H] + arrived(ru, c)
        grad[c, H:TILE - H] = own[c, H:TILE - H]
        grad[c, TILE - H:] = own[c, TILE - H:] + arrived(rd, c)
    copies = store(((grad, grad_out),), outs)
    left = jnp.where(low, grad[0, :, :LANE], half_turn(grad[1, :, :LANE]))
    right = jnp.where(low, half_turn(grad[0, :, 2 * LANE:]), grad[1, :, 2 * LANE:])
    near[...] = choose(right, left)
    far[...] = choose(left, right)
    finish(copies)


def last_kernel(obj, grad, probe, near, far, mine, other, out, out_probe, *inner):
    *inner, sems = inner
    wait = fetch((obj, grad, probe), inner, sems)
    obj, grad, probe = inner
    low = lanes()
    west, east = choose(far[...], near[...]), choose(near[...], far[...])
    wait(*range(3))
    for c in range(2):
        w = half_turn(west) if c == 0 else west
        e = east if c == 0 else half_turn(east)
        x = obj[c, :, :LANE] - object_step * (grad[c, :, :LANE] + w)
        y = obj[c, :, LANE:2 * LANE] - object_step * grad[c, :, LANE:2 * LANE]
        z = obj[c, :, 2 * LANE:] - object_step * (grad[c, :, 2 * LANE:] + e)
        x, y, z = half_turn(x), half_turn(y), half_turn(z)
        out[c, :, :LANE] = jnp.where(low, x, y)
        out[c, :, LANE:] = jnp.where(low, y, z)
    new_probe(lax.rem(lax.axis_index("col"), 2), probe, mine, other, out_probe)


VM = pl.BlockSpec(memory_space=pltpu.VMEM)
HBM = pl.BlockSpec(memory_space=pltpu.HBM)


def call(kernel, outs, name, limit=SMALL_LIMIT, specs=(), places=(), scratch=()):
    def run(*args):
        held = list(specs) or [VM] * len(args)
        inner = [
            (pltpu.VMEM if x.dtype != jnp.int32 else pltpu.SMEM)(x.shape, x.dtype)
            for x, s in zip(args, held) if s is HBM
        ]
        if inner:
            inner.append(pltpu.SemaphoreType.DMA((len(inner),)))
        return pl.pallas_call(
            kernel,
            out_shape=[jax.ShapeDtypeStruct(s, f32) for s in outs],
            in_specs=held,
            out_specs=list(places) or [VM] * len(outs),
            scratch_shapes=list(scratch) + inner,
            compiler_params=pltpu.CompilerParams(vmem_limit_bytes=limit),
            name=name,
        )(*args)

    return run


def shift(x, axis, step):
    count = lax.axis_size(axis)
    pairs = [(i, i + step) for i in range(count) if 0 <= i + step < count]
    return lax.ppermute(x, axis, pairs)


def exchange(x, mask):
    return lax.ppermute(x, RC, [(i, i ^ mask) for i in range(256)])


def columns(near, far):
    count = lax.axis_size("col")
    pairs = [(i, i + 1) for i in range(1, count - 1, 2)]
    pairs += [(j, i) for i, j in pairs]
    return exchange(near, BIT_CORE), lax.ppermute(far, "col", pairs)


def groups(mask):
    members = [i for i in range(256) if i & ~mask == 0]
    return [[base | i for i in members] for base in range(256) if base & mask == 0]


WIDE = BIT_Y | BIT_ZLO | BIT_X
COUNT = 32
CHUNK = 1024 // COUNT


def scatter(keep, send):
    x = keep + exchange(send, BIT_CORE)
    x = lax.all_to_all(x, RC, 0, 0, axis_index_groups=groups(WIDE), tiled=True)
    x = x.reshape(COUNT, CHUNK, LANE).sum(axis=0)
    return x, exchange(x, 2), exchange(x, 4), exchange(x, 6)


def gather(x, *early):
    x = lax.all_to_all(x, RC, 0, 0, axis_index_groups=groups(WIDE), tiled=True)
    x, early = lax.optimization_barrier((x, early))
    return x, exchange(x, BIT_CORE), *early


def local(object_field, probe, amplitudes, offsets):
    table = tables()
    sides = call(sides_kernel, [(TILE, LANE)] * 2, "sides")(object_field)
    mid, top, bottom = call(
        rows_kernel, [(2, TILE, SPAN)] + [(2, H, SPAN)] * 2, "rows"
    )(object_field, *columns(*sides))
    up = shift(bottom, "row", 1)
    down = shift(top, "row", -1)

    halves = [(1024, LANE)] * 2
    held = [pltpu.VMEM((2, SPAN + 8, SPAN), f32)] * 2 + [pltpu.VMEM((2, SPAN + 8, F), f32)]
    held += [pltpu.VMEM((8, F), f32)] + [pltpu.VMEM((1024, LANE), f32)] * 2
    keep, send, su, sd, own = call(
        functools.partial(frame_kernel, True),
        halves + [(2 * B + 8, F)] * 2 + [(2, SPAN, SPAN)],
        "frame1",
        VMEM_LIMIT,
        [HBM] * 7,
        [HBM] * 5,
        held + [pltpu.SemaphoreType.DMA((10,))],
    )(up, mid, down, offsets, probe, amplitudes, table)
    ru = shift(sd, "row", 1)
    rd = shift(su, "row", -1)
    total, ci, cm, co = call(
        bands_kernel,
        [(1024, LANE)] + [(2, SPAN, B)] * 3,
        "bands",
        specs=[VM] * 4 + [HBM] * 3,
        places=[VM] + [HBM] * 3,
        scratch=[pltpu.VMEM((2, SPAN, B), f32)] * 3 + [pltpu.SemaphoreType.DMA((3,))],
    )(*scatter(keep, send), own, ru, rd)
    mine, other, di, do = gather(total, *columns(ci, co))

    keep, send, su, sd, own, obj, probe = call(
        functools.partial(frame_kernel, False),
        halves + [(2 * H + 8, F)] * 2 + [(2, TILE, SPAN)] * 2 + [(2, M, F, F)],
        "frame2",
        VMEM_LIMIT,
        [HBM] * 14,
        [HBM] * 7,
        held + [pltpu.SemaphoreType.DMA((13,)), pltpu.VMEM((2, M, F, F), f32)],
    )(up, mid, down, offsets, ci, cm, co, di, do, probe, mine, other, amplitudes, table)
    ru = shift(sd, "row", 1)
    rd = shift(su, "row", -1)
    total, grad, near, far = call(
        last_bands_kernel,
        [(1024, LANE), (2, TILE, SPAN)] + [(TILE, LANE)] * 2,
        "last_bands",
        specs=[VM] * 4 + [HBM] * 3,
        places=[VM, HBM, VM, VM],
        scratch=[pltpu.VMEM((2, TILE, SPAN), f32), pltpu.SemaphoreType.DMA((1,))],
    )(*scatter(keep, send), own, ru, rd)
    mine, other, near, far = gather(total, *columns(near, far))
    return tuple(
        call(
            last_kernel,
            [(2, TILE, TILE), (2, M, F, F)],
            "last",
            specs=[HBM] * 3 + [VM] * 4,
        )(obj, grad, probe, near, far, mine, other)
    )


def solution(mesh):
    return jax.shard_map(
        local,
        mesh=mesh,
        in_specs=(
            P(None, "row", "col"),
            P(),
            P("row", "col", None, None, None),
            P("row", "col", None, None),
        ),
        out_specs=(P(None, "row", "col"), P()),
        check_vma=False,
    )
```

```python
import functools
import math

import jax
import jax.numpy as jnp
import ml_dtypes
import numpy as np
from jax import lax
from jax.experimental import pallas as pl
from jax.experimental.pallas import tpu as pltpu
from jax.sharding import PartitionSpec as P

H = 64
F = 256
M = 2
TILE = 256
SPAN = TILE + 2 * H
B = 2 * H
object_step = 0.25
probe_step = 4.0
RC = ("row", "col")
BIT_Y, BIT_ZLO, BIT_X, BIT_ZHI, BIT_CORE = 192, 32, 24, 6, 1

f32 = jnp.float32
bf16 = jnp.bfloat16
VMEM_LIMIT = 56 * 1024 * 1024
SMALL_LIMIT = 24 * 1024 * 1024
BANDS_LIMIT = 53 * 1024 * 1024


def tables():
    counter = np.arange(F)
    angle = -2.0 * math.pi / F * (counter[:, None] * counter[None, :] % F)
    out = []
    for table in (np.cos(angle) / math.sqrt(F), np.sin(angle) / math.sqrt(F)):
        high = table.astype(np.float32).astype(ml_dtypes.bfloat16)
        low = (table - high.astype(np.float64)).astype(np.float32).astype(ml_dtypes.bfloat16)
        out += [high, low]
    return np.concatenate(out, axis=0)


def blocks(table):
    rh, rl, ih, il = (table[k * F:(k + 1) * F, :] for k in range(4))

    def block(re, im, under):
        return jnp.concatenate(
            [jnp.concatenate([re, im], axis=1), jnp.concatenate([under, re], axis=1)], axis=0)

    return (block(rh, ih, -ih), block(rl, il, -il)), (block(rh, -ih, ih), block(rl, -il, il))


def split(x):
    high = x.astype(bf16)
    return high, (x - high.astype(f32)).astype(bf16)


def dot(a, b):
    return jnp.dot(a, b, preferred_element_type=f32)


def product(left, right):
    return dot(left[0], right[0]) + (dot(left[0], right[1]) + dot(left[1], right[0]))


LANE = 128


def lanes():
    return lax.broadcasted_iota(jnp.int32, (TILE, LANE), 1) < H


def half_turn(x):
    return pltpu.roll(x, H, 1)


def core_index():
    return lax.rem(lax.axis_index("col"), 2)


def choose(x, y):
    return jnp.where(core_index() == 0, x, y)


def sides_kernel(obj, inner, outer):
    low = lanes()
    left = jnp.where(low, obj[0, :, :LANE], half_turn(obj[1, :, :LANE]))
    right = jnp.where(low, half_turn(obj[0, :, LANE:]), obj[1, :, LANE:])
    inner[...] = choose(right, left)
    outer[...] = choose(left, right)


def rows_kernel(obj, inner, outer, mid, top, bottom):
    low = lanes()
    west, east = choose(outer[...], inner[...]), choose(inner[...], outer[...])
    for c in range(2):
        x, y = half_turn(obj[c, :, :LANE]), half_turn(obj[c, :, LANE:])
        w = west if c == 0 else half_turn(west)
        e = half_turn(east) if c == 0 else east
        for k, part in enumerate((jnp.where(low, w, x), jnp.where(low, x, y), jnp.where(low, y, e))):
            s = slice(k * LANE, (k + 1) * LANE)
            mid[c, :, s] = part
            top[c, :, s] = part[:H]
            bottom[c, :, s] = part[TILE - H:]


def fetch(refs, scratch, sems):
    copies = [pltpu.make_async_copy(r, t, sems.at[k]) for k, (r, t) in enumerate(zip(refs, scratch))]
    for copy in copies:
        copy.start()

    def wait(*which):
        for k in which:
            copies[k].wait()

    return wait


def store(pairs, sems):
    copies = [pltpu.make_async_copy(x, y, sems.at[k]) for k, (x, y) in enumerate(pairs)]
    for copy in copies:
        copy.start()
    return copies


def finish(copies):
    for copy in copies:
        copy.wait()


def frame_kernel(first, *refs):
    count = 7 if first else 14
    arrays, refs = refs[:count], refs[count:]
    if first:
        *stores, su, sd, own = refs[:5]
        ext, canvas, raw, head, keep, send, outs, *inner, sems = refs[5:]
        up, mid, down, off, probe, amps, table = inner
    else:
        *stores, su, sd, own, obj, probe_out = refs[:7]
        ext, canvas, raw, head, keep, send, outs, probe, *inner, sems = refs[7:]
        up, mid, down, off, ci, cm, co, di, do, probe_in, mine, other, amps, table = inner
    wait = fetch(arrays, inner, sems)
    canvas[...] = jnp.zeros(canvas.shape, f32)
    raw[...] = jnp.zeros(raw.shape, f32)
    wait(*range(4 if first else 9))
    o0 = off[0, 0, 0, 0]
    o1 = off[0, 0, 0, 1]
    row = lax.axis_index("row")
    col = lax.axis_index("col")
    core = lax.rem(col, 2)
    rest = lax.rem(o0, 8)
    base = pl.multiple_of(o0 - rest, 8)
    patch = []
    copies = []
    for c in range(2):
        whole = jnp.concatenate([up[c], mid[c], down[c]], axis=0)
        if not first:
            near, far = ci[c] + di[c], co[c] + do[c]
            grad = jnp.concatenate([choose(far, near), cm[c], choose(near, far)], axis=1)
            i = lax.broadcasted_iota(jnp.int32, (SPAN, SPAN), 0) + (row * TILE - H)
            j = lax.broadcasted_iota(jnp.int32, (SPAN, SPAN), 1) + (col * TILE - H)
            inside = (i >= 0) & (i < lax.axis_size("row") * TILE) & (j >= 0) & (
                j < lax.axis_size("col") * TILE)
            whole = jnp.where(inside, whole - object_step * grad, 0.0)
        ext[c, :SPAN, :] = whole
        ext[c, SPAN:, :] = jnp.zeros((8, SPAN), f32)
        rows = pltpu.roll(ext[c, pl.ds(base, F + 8), :], SPAN - o1, 1)[:, :F]
        patch.append(pltpu.roll(rows, F + 8 - rest, 0)[:F])
    pr, pi = patch
    if first:
        wait(4, 5, 6)
    else:
        wait(*range(9, 14))
        new_probe(core, probe_in, mine, other, probe)
        copies += store(
            ((ext.at[0, H:H + TILE], obj.at[0]), (ext.at[1, H:H + TILE], obj.at[1]),
             (probe, probe_out)), outs.at[10:13])
    right, left = blocks(table)
    wave = jnp.concatenate(
        [
            jnp.concatenate(
                [
                    probe[0, m] * pr - probe[1, m] * pi,
                    probe[0, m] * pi + probe[1, m] * pr,
                ],
                axis=1,
            )
            for m in range(M)
        ],
        axis=0,
    )
    x = product(split(wave), right)
    x = jnp.concatenate(
        [jnp.concatenate([x[m * F:(m + 1) * F, p * F:(p + 1) * F] for m in range(M)], axis=1)
         for p in range(2)], axis=0)
    x = product(left, split(x))
    square = x[:F] * x[:F] + x[F:] * x[F:]
    intensity = square[:, :F] + square[:, F:]
    factor = 1.0 - amps[0, 0, 0] * lax.rsqrt(intensity + 1.0)
    factor = jnp.concatenate([factor, factor], axis=1)
    x = jnp.concatenate([x[:F] * factor, x[F:] * factor], axis=0)
    x = product(right, split(x))
    x = jnp.concatenate(
        [jnp.concatenate([x[p * F:(p + 1) * F, m * F:(m + 1) * F] for p in range(2)], axis=1)
         for m in range(M)], axis=0)
    x = product(split(x), left)
    ore = jnp.zeros((F, F), f32)
    oim = jnp.zeros((F, F), f32)
    for m in range(M):
        br, bi = x[m * F:(m + 1) * F, :F], x[m * F:(m + 1) * F, F:]
        qr, qi = probe[0, m], probe[1, m]
        ore = ore + (qr * br + qi * bi)
        oim = oim + (qr * bi - qi * br)
        for p, term in enumerate((pr * br + pi * bi, pr * bi - pi * br)):
            s = slice((p * M + m) * F, (p * M + m + 1) * F)
            keep[s, :] = jnp.where(core == 0, term[:, :LANE], term[:, LANE:])
            send[s, :] = jnp.where(core == 0, term[:, LANE:], term[:, :LANE])
    copies += store(zip((keep, send), stores), outs.at[8:10])
    edge = (su.shape[0] - 8) // 2
    skip = (SPAN - own.shape[1]) // 2
    head[...] = jnp.full((8, F), o1.astype(f32))
    for c, value in enumerate((ore, oim)):
        value = jnp.concatenate([value, jnp.zeros((8, F), f32)], axis=0)
        value = pltpu.roll(value, rest, 0)
        raw[c, pl.ds(base, F + 8), :] = value
        s = slice(c * edge, (c + 1) * edge)
        copies += store(
            ((raw.at[c, :edge], su.at[s]), (raw.at[c, SPAN - edge:SPAN], sd.at[s])),
            outs.at[2 * c:2 * c + 2])
        canvas[c, pl.ds(base, F + 8), :] = shifted(value, o1)
        copies += store(((canvas.at[c, skip:SPAN - skip], own.at[c]),), outs.at[4 + c:5 + c])
    copies += store(((head, su.at[2 * edge:]), (head, sd.at[2 * edge:])), outs.at[6:8])
    finish(copies)


def shifted(value, columns):
    value = jnp.concatenate([value, jnp.zeros((value.shape[0], SPAN - F), f32)], axis=1)
    return pltpu.roll(value, columns, 1)


def arrived(strip, c):
    edge = (strip.shape[0] - 8) // 2
    columns = jnp.max(strip[2 * edge:, :LANE]).astype(jnp.int32)
    return shifted(strip[c * edge:(c + 1) * edge, :], columns)


def new_probe(core, probe, mine, other, out):
    coeff = probe_step / (lax.axis_size("row") * lax.axis_size("col"))
    for q in range(4):
        s = slice(q * F, (q + 1) * F)
        x, y = mine[s, :], other[s, :]
        total = jnp.concatenate(
            [jnp.where(core == 0, x, y), jnp.where(core == 0, y, x)], axis=1)
        out[q // 2, q % 2] = probe[q // 2, q % 2] - coeff * total


def spread(parts, out):
    a, b, c, d = parts
    total = (a[...] + b[...]) + (c[...] + d[...])
    rows = a.shape[0]
    for k in range(out.shape[0] // rows):
        out[k * rows:(k + 1) * rows, :] = total


def bands_kernel(p0, p1, p2, p3, own, ru, rd, total, ci, cm, co, ti, tm, to, outs, *inner):
    *inner, sems = inner
    wait = fetch((own, ru, rd), inner, sems)
    own, ru, rd = inner
    spread((p0, p1, p2, p3), total)
    wait(*range(3))
    for c in range(2):
        rows = jnp.concatenate(
            [own[c, :B] + arrived(ru, c), own[c, B:2 * B], own[c, 2 * B:] + arrived(rd, c)], axis=0)
        left, tm[c], right = rows[:, :B], rows[:, B:2 * B], rows[:, 2 * B:]
        ti[c] = choose(right, left)
        to[c] = choose(left, right)
    finish(store(zip((ti, to, tm), (ci, co, cm)), outs))


def last_bands_kernel(p0, p1, p2, p3, own, ru, rd, total, grad_out, near, far, grad, outs, *inner):
    *inner, sems = inner
    wait = fetch((own, ru, rd), inner, sems)
    own, ru, rd = inner
    spread((p0, p1, p2, p3), total)
    low = lanes()
    wait(*range(3))
    for c in range(2):
        grad[c, :H] = own[c, :H] + arrived(ru, c)
        grad[c, H:TILE - H] = own[c, H:TILE - H]
        grad[c, TILE - H:] = own[c, TILE - H:] + arrived(rd, c)
    copies = store(((grad, grad_out),), outs)
    left = jnp.where(low, grad[0, :, :LANE], half_turn(grad[1, :, :LANE]))
    right = jnp.where(low, half_turn(grad[0, :, 2 * LANE:]), grad[1, :, 2 * LANE:])
    near[...] = choose(right, left)
    far[...] = choose(left, right)
    finish(copies)


def last_kernel(obj, grad, probe, near, far, mine, other, out, out_probe, *inner):
    *inner, sems = inner
    wait = fetch((obj, grad, probe), inner, sems)
    obj, grad, probe = inner
    low = lanes()
    west, east = choose(far[...], near[...]), choose(near[...], far[...])
    wait(*range(3))
    for c in range(2):
        w = half_turn(west) if c == 0 else west
        e = east if c == 0 else half_turn(east)
        x = obj[c, :, :LANE] - object_step * (grad[c, :, :LANE] + w)
        y = obj[c, :, LANE:2 * LANE] - object_step * grad[c, :, LANE:2 * LANE]
        z = obj[c, :, 2 * LANE:] - object_step * (grad[c, :, 2 * LANE:] + e)
        x, y, z = half_turn(x), half_turn(y), half_turn(z)
        out[c, :, :LANE] = jnp.where(low, x, y)
        out[c, :, LANE:] = jnp.where(low, y, z)
    new_probe(lax.rem(lax.axis_index("col"), 2), probe, mine, other, out_probe)


VM = pl.BlockSpec(memory_space=pltpu.VMEM)
HBM = pl.BlockSpec(memory_space=pltpu.HBM)


def call(kernel, outs, name, limit=SMALL_LIMIT, specs=(), places=(), scratch=()):
    def run(*args):
        held = list(specs) or [VM] * len(args)
        inner = [
            (pltpu.VMEM if x.dtype != jnp.int32 else pltpu.SMEM)(x.shape, x.dtype)
            for x, s in zip(args, held) if s is HBM
        ]
        if inner:
            inner.append(pltpu.SemaphoreType.DMA((len(inner),)))
        return pl.pallas_call(
            kernel,
            out_shape=[jax.ShapeDtypeStruct(s, f32) for s in outs],
            in_specs=held,
            out_specs=list(places) or [VM] * len(outs),
            scratch_shapes=list(scratch) + inner,
            compiler_params=pltpu.CompilerParams(vmem_limit_bytes=limit),
            name=name,
        )(*args)

    return run


def shift(x, axis, step):
    count = lax.axis_size(axis)
    pairs = [(i, i + step) for i in range(count) if 0 <= i + step < count]
    return lax.ppermute(x, axis, pairs)


def exchange(x, mask):
    return lax.ppermute(x, RC, [(i, i ^ mask) for i in range(256)])


def columns(near, far):
    count = lax.axis_size("col")
    pairs = [(i, i + 1) for i in range(1, count - 1, 2)]
    pairs += [(j, i) for i, j in pairs]
    return exchange(near, BIT_CORE), lax.ppermute(far, "col", pairs)


def groups(mask):
    members = [i for i in range(256) if i & ~mask == 0]
    return [[base | i for i in members] for base in range(256) if base & mask == 0]


WIDE = BIT_Y | BIT_ZLO | BIT_X
COUNT = 32
CHUNK = 1024 // COUNT


def scatter(keep, send):
    x = keep + exchange(send, BIT_CORE)
    x = lax.all_to_all(x, RC, 0, 0, axis_index_groups=groups(WIDE), tiled=True)
    x = x.reshape(COUNT, CHUNK, LANE).sum(axis=0)
    return x, exchange(x, 2), exchange(x, 4), exchange(x, 6)


def gather(x, *early):
    x = lax.all_to_all(x, RC, 0, 0, axis_index_groups=groups(WIDE), tiled=True)
    x, early = lax.optimization_barrier((x, early))
    return x, exchange(x, BIT_CORE), *early


def local(object_field, probe, amplitudes, offsets):
    table = tables()
    sides = call(sides_kernel, [(TILE, LANE)] * 2, "sides")(object_field)
    mid, top, bottom = call(
        rows_kernel, [(2, TILE, SPAN)] + [(2, H, SPAN)] * 2, "rows"
    )(object_field, *columns(*sides))
    up = shift(bottom, "row", 1)
    down = shift(top, "row", -1)

    halves = [(1024, LANE)] * 2
    held = [pltpu.VMEM((2, SPAN + 8, SPAN), f32)] * 2 + [pltpu.VMEM((2, SPAN + 8, F), f32)]
    held += [pltpu.VMEM((8, F), f32)] + [pltpu.VMEM((1024, LANE), f32)] * 2
    keep, send, su, sd, own = call(
        functools.partial(frame_kernel, True),
        halves + [(2 * B + 8, F)] * 2 + [(2, SPAN, SPAN)],
        "frame1",
        VMEM_LIMIT,
        [HBM] * 7,
        [HBM] * 5,
        held + [pltpu.SemaphoreType.DMA((10,))],
    )(up, mid, down, offsets, probe, amplitudes, table)
    ru = shift(sd, "row", 1)
    rd = shift(su, "row", -1)
    total, ci, cm, co = call(
        bands_kernel,
        [(1024, LANE)] + [(2, SPAN, B)] * 3,
        "bands",
        BANDS_LIMIT,
        specs=[VM] * 4 + [HBM] * 3,
        places=[VM] + [HBM] * 3,
        scratch=[pltpu.VMEM((2, SPAN, B), f32)] * 3 + [pltpu.SemaphoreType.DMA((3,))],
    )(*scatter(keep, send), own, ru, rd)
    mine, other, di, do = gather(total, *columns(ci, co))

    keep, send, su, sd, own, obj, probe = call(
        functools.partial(frame_kernel, False),
        halves + [(2 * H + 8, F)] * 2 + [(2, TILE, SPAN)] * 2 + [(2, M, F, F)],
        "frame2",
        VMEM_LIMIT,
        [HBM] * 14,
        [HBM] * 7,
        held + [pltpu.SemaphoreType.DMA((13,)), pltpu.VMEM((2, M, F, F), f32)],
    )(up, mid, down, offsets, ci, cm, co, di, do, probe, mine, other, amplitudes, table)
    ru = shift(sd, "row", 1)
    rd = shift(su, "row", -1)
    total, grad, near, far = call(
        last_bands_kernel,
        [(1024, LANE), (2, TILE, SPAN)] + [(TILE, LANE)] * 2,
        "last_bands",
        BANDS_LIMIT,
        specs=[VM] * 4 + [HBM] * 3,
        places=[VM, HBM, VM, VM],
        scratch=[pltpu.VMEM((2, TILE, SPAN), f32), pltpu.SemaphoreType.DMA((1,))],
    )(*scatter(keep, send), own, ru, rd)
    mine, other, near, far = gather(total, *columns(near, far))
    return tuple(
        call(
            last_kernel,
            [(2, TILE, TILE), (2, M, F, F)],
            "last",
            specs=[HBM] * 3 + [VM] * 4,
        )(obj, grad, probe, near, far, mine, other)
    )


def solution(mesh):
    return jax.shard_map(
        local,
        mesh=mesh,
        in_specs=(
            P(None, "row", "col"),
            P(),
            P("row", "col", None, None, None),
            P("row", "col", None, None),
        ),
        out_specs=(P(None, "row", "col"), P()),
        check_vma=False,
    )
```

```python
import functools
import math

import jax
import jax.numpy as jnp
import ml_dtypes
import numpy as np
from jax import lax
from jax.experimental import pallas as pl
from jax.experimental.pallas import tpu as pltpu
from jax.sharding import PartitionSpec as P

H = 64
F = 256
M = 2
TILE = 256
SPAN = TILE + 2 * H
B = 2 * H
object_step = 0.25
probe_step = 4.0
RC = ("row", "col")
BIT_Y, BIT_ZLO, BIT_X, BIT_ZHI, BIT_CORE = 192, 32, 24, 6, 1

f32 = jnp.float32
bf16 = jnp.bfloat16
VMEM_LIMIT = 56 * 1024 * 1024
SMALL_LIMIT = 24 * 1024 * 1024
LAST_LIMIT = 53 * 1024 * 1024


def tables():
    counter = np.arange(F)
    angle = -2.0 * math.pi / F * (counter[:, None] * counter[None, :] % F)
    out = []
    for table in (np.cos(angle) / math.sqrt(F), np.sin(angle) / math.sqrt(F)):
        high = table.astype(np.float32).astype(ml_dtypes.bfloat16)
        low = (table - high.astype(np.float64)).astype(np.float32).astype(ml_dtypes.bfloat16)
        out += [high, low]
    return np.concatenate(out, axis=0)


def blocks(table):
    rh, rl, ih, il = (table[k * F:(k + 1) * F, :] for k in range(4))

    def block(re, im, under):
        return jnp.concatenate(
            [jnp.concatenate([re, im], axis=1), jnp.concatenate([under, re], axis=1)], axis=0)

    return (block(rh, ih, -ih), block(rl, il, -il)), (block(rh, -ih, ih), block(rl, -il, il))


def split(x):
    high = x.astype(bf16)
    return high, (x - high.astype(f32)).astype(bf16)


def dot(a, b):
    return jnp.dot(a, b, preferred_element_type=f32)


def product(left, right):
    return dot(left[0], right[0]) + (dot(left[0], right[1]) + dot(left[1], right[0]))


LANE = 128


def lanes():
    return lax.broadcasted_iota(jnp.int32, (TILE, LANE), 1) < H


def half_turn(x):
    return pltpu.roll(x, H, 1)


def core_index():
    return lax.rem(lax.axis_index("col"), 2)


def choose(x, y):
    return jnp.where(core_index() == 0, x, y)


def sides_kernel(obj, inner, outer):
    low = lanes()
    left = jnp.where(low, obj[0, :, :LANE], half_turn(obj[1, :, :LANE]))
    right = jnp.where(low, half_turn(obj[0, :, LANE:]), obj[1, :, LANE:])
    inner[...] = choose(right, left)
    outer[...] = choose(left, right)


def rows_kernel(obj, inner, outer, mid, top, bottom):
    low = lanes()
    west, east = choose(outer[...], inner[...]), choose(inner[...], outer[...])
    for c in range(2):
        x, y = half_turn(obj[c, :, :LANE]), half_turn(obj[c, :, LANE:])
        w = west if c == 0 else half_turn(west)
        e = half_turn(east) if c == 0 else east
        for k, part in enumerate((jnp.where(low, w, x), jnp.where(low, x, y), jnp.where(low, y, e))):
            s = slice(k * LANE, (k + 1) * LANE)
            mid[c, :, s] = part
            top[c, :, s] = part[:H]
            bottom[c, :, s] = part[TILE - H:]


def fetch(refs, scratch, sems):
    copies = [pltpu.make_async_copy(r, t, sems.at[k]) for k, (r, t) in enumerate(zip(refs, scratch))]
    for copy in copies:
        copy.start()

    def wait(*which):
        for k in which:
            copies[k].wait()

    return wait


def store(pairs, sems):
    copies = [pltpu.make_async_copy(x, y, sems.at[k]) for k, (x, y) in enumerate(pairs)]
    for copy in copies:
        copy.start()
    return copies


def finish(copies):
    for copy in copies:
        copy.wait()


def frame_kernel(first, *refs):
    count = 7 if first else 14
    arrays, refs = refs[:count], refs[count:]
    if first:
        *stores, su, sd, own = refs[:5]
        ext, canvas, raw, head, keep, send, outs, *inner, sems = refs[5:]
        up, mid, down, off, probe, amps, table = inner
    else:
        *stores, su, sd, own, obj, probe_out = refs[:7]
        ext, canvas, raw, head, keep, send, outs, probe, *inner, sems = refs[7:]
        up, mid, down, off, ci, cm, co, di, do, probe_in, mine, other, amps, table = inner
    wait = fetch(arrays, inner, sems)
    canvas[...] = jnp.zeros(canvas.shape, f32)
    raw[...] = jnp.zeros(raw.shape, f32)
    wait(*range(4 if first else 9))
    o0 = off[0, 0, 0, 0]
    o1 = off[0, 0, 0, 1]
    row = lax.axis_index("row")
    col = lax.axis_index("col")
    core = lax.rem(col, 2)
    rest = lax.rem(o0, 8)
    base = pl.multiple_of(o0 - rest, 8)
    patch = []
    copies = []
    for c in range(2):
        whole = jnp.concatenate([up[c], mid[c], down[c]], axis=0)
        if not first:
            near, far = ci[c] + di[c], co[c] + do[c]
            grad = jnp.concatenate([choose(far, near), cm[c], choose(near, far)], axis=1)
            i = lax.broadcasted_iota(jnp.int32, (SPAN, SPAN), 0) + (row * TILE - H)
            j = lax.broadcasted_iota(jnp.int32, (SPAN, SPAN), 1) + (col * TILE - H)
            inside = (i >= 0) & (i < lax.axis_size("row") * TILE) & (j >= 0) & (
                j < lax.axis_size("col") * TILE)
            whole = jnp.where(inside, whole - object_step * grad, 0.0)
        ext[c, :SPAN, :] = whole
        ext[c, SPAN:, :] = jnp.zeros((8, SPAN), f32)
        rows = pltpu.roll(ext[c, pl.ds(base, F + 8), :], SPAN - o1, 1)[:, :F]
        patch.append(pltpu.roll(rows, F + 8 - rest, 0)[:F])
    pr, pi = patch
    if first:
        wait(4, 5, 6)
    else:
        wait(*range(9, 14))
        new_probe(core, probe_in, mine, other, probe)
        copies += store(
            ((ext.at[0, H:H + TILE], obj.at[0]), (ext.at[1, H:H + TILE], obj.at[1]),
             (probe, probe_out)), outs.at[10:13])
    right, left = blocks(table)
    wave = jnp.concatenate(
        [
            jnp.concatenate(
                [
                    probe[0, m] * pr - probe[1, m] * pi,
                    probe[0, m] * pi + probe[1, m] * pr,
                ],
                axis=1,
            )
            for m in range(M)
        ],
        axis=0,
    )
    x = product(split(wave), right)
    x = jnp.concatenate(
        [jnp.concatenate([x[m * F:(m + 1) * F, p * F:(p + 1) * F] for m in range(M)], axis=1)
         for p in range(2)], axis=0)
    x = product(left, split(x))
    square = x[:F] * x[:F] + x[F:] * x[F:]
    intensity = square[:, :F] + square[:, F:]
    factor = 1.0 - amps[0, 0, 0] * lax.rsqrt(intensity + 1.0)
    factor = jnp.concatenate([factor, factor], axis=1)
    x = jnp.concatenate([x[:F] * factor, x[F:] * factor], axis=0)
    x = product(right, split(x))
    x = jnp.concatenate(
        [jnp.concatenate([x[p * F:(p + 1) * F, m * F:(m + 1) * F] for p in range(2)], axis=1)
         for m in range(M)], axis=0)
    x = product(split(x), left)
    ore = jnp.zeros((F, F), f32)
    oim = jnp.zeros((F, F), f32)
    for m in range(M):
        br, bi = x[m * F:(m + 1) * F, :F], x[m * F:(m + 1) * F, F:]
        qr, qi = probe[0, m], probe[1, m]
        ore = ore + (qr * br + qi * bi)
        oim = oim + (qr * bi - qi * br)
        for p, term in enumerate((pr * br + pi * bi, pr * bi - pi * br)):
            s = slice((p * M + m) * F, (p * M + m + 1) * F)
            keep[s, :] = jnp.where(core == 0, term[:, :LANE], term[:, LANE:])
            send[s, :] = jnp.where(core == 0, term[:, LANE:], term[:, :LANE])
    copies += store(zip((keep, send), stores), outs.at[8:10])
    edge = (su.shape[0] - 8) // 2
    skip = (SPAN - own.shape[1]) // 2
    head[...] = jnp.full((8, F), o1.astype(f32))
    for c, value in enumerate((ore, oim)):
        value = jnp.concatenate([value, jnp.zeros((8, F), f32)], axis=0)
        value = pltpu.roll(value, rest, 0)
        raw[c, pl.ds(base, F + 8), :] = value
        s = slice(c * edge, (c + 1) * edge)
        copies += store(
            ((raw.at[c, :edge], su.at[s]), (raw.at[c, SPAN - edge:SPAN], sd.at[s])),
            outs.at[2 * c:2 * c + 2])
        canvas[c, pl.ds(base, F + 8), :] = shifted(value, o1)
        copies += store(((canvas.at[c, skip:SPAN - skip], own.at[c]),), outs.at[4 + c:5 + c])
    copies += store(((head, su.at[2 * edge:]), (head, sd.at[2 * edge:])), outs.at[6:8])
    finish(copies)


def shifted(value, columns):
    value = jnp.concatenate([value, jnp.zeros((value.shape[0], SPAN - F), f32)], axis=1)
    return pltpu.roll(value, columns, 1)


def arrived(strip, c):
    edge = (strip.shape[0] - 8) // 2
    columns = jnp.max(strip[2 * edge:, :LANE]).astype(jnp.int32)
    return shifted(strip[c * edge:(c + 1) * edge, :], columns)


def new_probe(core, probe, mine, other, out):
    coeff = probe_step / (lax.axis_size("row") * lax.axis_size("col"))
    for q in range(4):
        s = slice(q * F, (q + 1) * F)
        x, y = mine[s, :], other[s, :]
        total = jnp.concatenate(
            [jnp.where(core == 0, x, y), jnp.where(core == 0, y, x)], axis=1)
        out[q // 2, q % 2] = probe[q // 2, q % 2] - coeff * total


def spread(parts, out):
    a, b, c, d = parts
    total = (a[...] + b[...]) + (c[...] + d[...])
    rows = a.shape[0]
    for k in range(out.shape[0] // rows):
        out[k * rows:(k + 1) * rows, :] = total


def bands_kernel(p0, p1, p2, p3, own, ru, rd, total, ci, cm, co, ti, tm, to, outs, *inner):
    *inner, sems = inner
    wait = fetch((own, ru, rd), inner, sems)
    own, ru, rd = inner
    spread((p0, p1, p2, p3), total)
    wait(*range(3))
    for c in range(2):
        rows = jnp.concatenate(
            [own[c, :B] + arrived(ru, c), own[c, B:2 * B], own[c, 2 * B:] + arrived(rd, c)], axis=0)
        left, tm[c], right = rows[:, :B], rows[:, B:2 * B], rows[:, 2 * B:]
        ti[c] = choose(right, left)
        to[c] = choose(left, right)
    finish(store(zip((ti, to, tm), (ci, co, cm)), outs))


def last_bands_kernel(p0, p1, p2, p3, own, ru, rd, total, grad_out, near, far, grad, outs, *inner):
    *inner, sems = inner
    wait = fetch((own, ru, rd), inner, sems)
    own, ru, rd = inner
    spread((p0, p1, p2, p3), total)
    low = lanes()
    wait(*range(3))
    for c in range(2):
        grad[c, :H] = own[c, :H] + arrived(ru, c)
        grad[c, H:TILE - H] = own[c, H:TILE - H]
        grad[c, TILE - H:] = own[c, TILE - H:] + arrived(rd, c)
    copies = store(((grad, grad_out),), outs)
    left = jnp.where(low, grad[0, :, :LANE], half_turn(grad[1, :, :LANE]))
    right = jnp.where(low, half_turn(grad[0, :, 2 * LANE:]), grad[1, :, 2 * LANE:])
    near[...] = choose(right, left)
    far[...] = choose(left, right)
    finish(copies)


def last_kernel(obj, grad, probe, near, far, mine, other, out, out_probe, *inner):
    *inner, sems = inner
    wait = fetch((obj, grad, probe), inner, sems)
    obj, grad, probe = inner
    low = lanes()
    west, east = choose(far[...], near[...]), choose(near[...], far[...])
    wait(*range(3))
    for c in range(2):
        w = half_turn(west) if c == 0 else west
        e = east if c == 0 else half_turn(east)
        x = obj[c, :, :LANE] - object_step * (grad[c, :, :LANE] + w)
        y = obj[c, :, LANE:2 * LANE] - object_step * grad[c, :, LANE:2 * LANE]
        z = obj[c, :, 2 * LANE:] - object_step * (grad[c, :, 2 * LANE:] + e)
        x, y, z = half_turn(x), half_turn(y), half_turn(z)
        out[c, :, :LANE] = jnp.where(low, x, y)
        out[c, :, LANE:] = jnp.where(low, y, z)
    new_probe(lax.rem(lax.axis_index("col"), 2), probe, mine, other, out_probe)


VM = pl.BlockSpec(memory_space=pltpu.VMEM)
HBM = pl.BlockSpec(memory_space=pltpu.HBM)


def call(kernel, outs, name, limit=SMALL_LIMIT, specs=(), places=(), scratch=()):
    def run(*args):
        held = list(specs) or [VM] * len(args)
        inner = [
            (pltpu.VMEM if x.dtype != jnp.int32 else pltpu.SMEM)(x.shape, x.dtype)
            for x, s in zip(args, held) if s is HBM
        ]
        if inner:
            inner.append(pltpu.SemaphoreType.DMA((len(inner),)))
        return pl.pallas_call(
            kernel,
            out_shape=[jax.ShapeDtypeStruct(s, f32) for s in outs],
            in_specs=held,
            out_specs=list(places) or [VM] * len(outs),
            scratch_shapes=list(scratch) + inner,
            compiler_params=pltpu.CompilerParams(vmem_limit_bytes=limit),
            name=name,
        )(*args)

    return run


def shift(x, axis, step):
    count = lax.axis_size(axis)
    pairs = [(i, i + step) for i in range(count) if 0 <= i + step < count]
    return lax.ppermute(x, axis, pairs)


def exchange(x, mask):
    return lax.ppermute(x, RC, [(i, i ^ mask) for i in range(256)])


def columns(near, far):
    count = lax.axis_size("col")
    pairs = [(i, i + 1) for i in range(1, count - 1, 2)]
    pairs += [(j, i) for i, j in pairs]
    return exchange(near, BIT_CORE), lax.ppermute(far, "col", pairs)


def groups(mask):
    members = [i for i in range(256) if i & ~mask == 0]
    return [[base | i for i in members] for base in range(256) if base & mask == 0]


WIDE = BIT_Y | BIT_ZLO | BIT_X
COUNT = 32
CHUNK = 1024 // COUNT


def scatter(keep, send):
    x = keep + exchange(send, BIT_CORE)
    x = lax.all_to_all(x, RC, 0, 0, axis_index_groups=groups(WIDE), tiled=True)
    x = x.reshape(COUNT, CHUNK, LANE).sum(axis=0)
    return x, exchange(x, 2), exchange(x, 4), exchange(x, 6)


def gather(x, *early):
    x = lax.all_to_all(x, RC, 0, 0, axis_index_groups=groups(WIDE), tiled=True)
    x, early = lax.optimization_barrier((x, early))
    return x, exchange(x, BIT_CORE), *early


def local(object_field, probe, amplitudes, offsets):
    table = tables()
    sides = call(sides_kernel, [(TILE, LANE)] * 2, "sides")(object_field)
    mid, top, bottom = call(
        rows_kernel, [(2, TILE, SPAN)] + [(2, H, SPAN)] * 2, "rows"
    )(object_field, *columns(*sides))
    up = shift(bottom, "row", 1)
    down = shift(top, "row", -1)

    halves = [(1024, LANE)] * 2
    held = [pltpu.VMEM((2, SPAN + 8, SPAN), f32)] * 2 + [pltpu.VMEM((2, SPAN + 8, F), f32)]
    held += [pltpu.VMEM((8, F), f32)] + [pltpu.VMEM((1024, LANE), f32)] * 2
    keep, send, su, sd, own = call(
        functools.partial(frame_kernel, True),
        halves + [(2 * B + 8, F)] * 2 + [(2, SPAN, SPAN)],
        "frame1",
        VMEM_LIMIT,
        [HBM] * 7,
        [HBM] * 5,
        held + [pltpu.SemaphoreType.DMA((10,))],
    )(up, mid, down, offsets, probe, amplitudes, table)
    ru = shift(sd, "row", 1)
    rd = shift(su, "row", -1)
    total, ci, cm, co = call(
        bands_kernel,
        [(1024, LANE)] + [(2, SPAN, B)] * 3,
        "bands",
        specs=[VM] * 4 + [HBM] * 3,
        places=[VM] + [HBM] * 3,
        scratch=[pltpu.VMEM((2, SPAN, B), f32)] * 3 + [pltpu.SemaphoreType.DMA((3,))],
    )(*scatter(keep, send), own, ru, rd)
    mine, other, di, do = gather(total, *columns(ci, co))

    keep, send, su, sd, own, obj, probe = call(
        functools.partial(frame_kernel, False),
        halves + [(2 * H + 8, F)] * 2 + [(2, TILE, SPAN)] * 2 + [(2, M, F, F)],
        "frame2",
        VMEM_LIMIT,
        [HBM] * 14,
        [HBM] * 7,
        held + [pltpu.SemaphoreType.DMA((13,)), pltpu.VMEM((2, M, F, F), f32)],
    )(up, mid, down, offsets, ci, cm, co, di, do, probe, mine, other, amplitudes, table)
    ru = shift(sd, "row", 1)
    rd = shift(su, "row", -1)
    total, grad, near, far = call(
        last_bands_kernel,
        [(1024, LANE), (2, TILE, SPAN)] + [(TILE, LANE)] * 2,
        "last_bands",
        specs=[VM] * 4 + [HBM] * 3,
        places=[VM, HBM, VM, VM],
        scratch=[pltpu.VMEM((2, TILE, SPAN), f32), pltpu.SemaphoreType.DMA((1,))],
    )(*scatter(keep, send), own, ru, rd)
    mine, other, near, far = gather(total, *columns(near, far))
    return tuple(
        call(
            last_kernel,
            [(2, TILE, TILE), (2, M, F, F)],
            "last",
            LAST_LIMIT,
            specs=[HBM] * 3 + [VM] * 4,
        )(obj, grad, probe, near, far, mine, other)
    )


def solution(mesh):
    return jax.shard_map(
        local,
        mesh=mesh,
        in_specs=(
            P(None, "row", "col"),
            P(),
            P("row", "col", None, None, None),
            P("row", "col", None, None),
        ),
        out_specs=(P(None, "row", "col"), P()),
        check_vma=False,
    )
```
